128 devices in a mesh: section: 2 (over y_lo), tensor: 8 (over x, y_hi), dp: 8 (over z, core).
Axes of the slice: x: 4, y: 4 (y_hi: 2, y_lo: 2; y = y_hi * 2 + y_lo), z: 4, core: 2. Of those that a mesh axis runs over, the one named last changes fastest.
Arguments:
- inputs: bfloat16 [2, 8, 512, 1024], P(None, 'dp', 'tensor'), may hold values from -6 to 6
- segments: int32 [2, 8, 512], P(None, 'dp'), may hold values from 0 to 7, as said below
- qkv_weight: bfloat16 [2, 3, 1024, 1024], P('section', None, None, 'tensor'), may hold values from -0.1875 to 0.1875
- qv_bias: bfloat16 [2, 2, 1024], P('section', None, 'tensor'), may hold values from -3 to 3
- out_weight: bfloat16 [2, 1024, 1024], P('section', 'tensor'), may hold values from -0.5 to 0.5
- out_bias: bfloat16 [2, 1024], P('section'), may hold values from -3 to 3
- gain_one: bfloat16 [2, 1024], P('section'), may hold values from 0.5 to 1.5
- shift_one: bfloat16 [2, 1024], P('section'), may hold values from -3 to 3
- up_weight: bfloat16 [2, 1024, 4096], P('section', None, 'tensor'), may hold values from -0.1875 to 0.1875
- up_bias: bfloat16 [2, 4096], P('section', 'tensor'), may hold values from -3 to 3
- down_weight: bfloat16 [2, 4096, 1024], P('section', 'tensor'), may hold values from -0.09375 to 0.09375
- down_bias: bfloat16 [2, 1024], P('section'), may hold values from -3 to 3
- gain_two: bfloat16 [2, 1024], P('section'), may hold values from 0.5 to 1.5
- shift_two: bfloat16 [2, 1024], P('section'), may hold values from -3 to 3
- cotangent: bfloat16 [2, 8, 512, 1024], P(None, 'dp', 'tensor'), may hold values from -6 to 6
Outputs:
- layer_outputs: bfloat16 [2, 2, 8, 512, 1024], P('section', None, 'dp', 'tensor')
- input_grads: bfloat16 [2, 2, 8, 512, 1024], P('section', None, 'dp', 'tensor')
- grad_qkv: float32 [2, 3, 1024, 1024], P('section', None, None, 'tensor')
- grad_qv_bias: float32 [2, 2, 1024], P('section', None, 'tensor')
- grad_out_weight: float32 [2, 1024, 1024], P('section', 'tensor')
- grad_out_bias: float32 [2, 1024], P('section')
- grad_gain_one: float32 [2, 1024], P('section')
- grad_shift_one: float32 [2, 1024], P('section')
- grad_up_weight: float32 [2, 1024, 4096], P('section', None, 'tensor')
- grad_up_bias: float32 [2, 4096], P('section', 'tensor')
- grad_down_weight: float32 [2, 4096, 1024], P('section', 'tensor')
- grad_down_bias: float32 [2, 1024], P('section')
- grad_gain_two: float32 [2, 1024], P('section')
- grad_shift_two: float32 [2, 1024], P('section')
The draws below stay inside these ranges and needn't reach their ends.
Inputs may be any that keep to these rules, and one draw needn't show every extreme that they name: `segments`: in every pack the numbers start at 0 at the first position and never fall, so each document is one run of positions; a position attends only to positions of its own document in its own pack.
All inputs are finite; a program needn't handle non-finite values.
Results may differ from the reference program's by a relative error of at most 0.028.
Values may be sent and summed in bfloat16 or wider, within the bound.
A program may use at most 128 MiB of HBM per device.

```python
import jax
import jax.numpy as jnp
from jax import lax

D = 1024
FF = 4096
HEADS = 16
HEAD_DIM = 64
SEQ = 512
MICRO = 2
PACKS_ALL = 8
LAYERS = 2
N_SECTION = 2


def draw_segments(key, part):
    key = jax.random.fold_in(key, 7)
    block_len = SEQ // 8
    first_key, second_key = jax.random.split(key)
    offsets = jax.random.randint(first_key, (MICRO, PACKS_ALL, 7), 0, block_len * 11 // 16)
    bounds = block_len * jnp.arange(1, 8, dtype=jnp.int32)[None, None, :] + offsets
    long_micro = jax.random.randint(second_key, (PACKS_ALL,), 0, MICRO)
    is_long = jnp.arange(MICRO, dtype=jnp.int32)[:, None] == long_micro[None, :]
    last_only = jnp.arange(7, dtype=jnp.int32) == 6
    keep_bound = jnp.where(is_long[:, :, None], last_only[None, None, :], True)
    positions = jnp.arange(SEQ, dtype=jnp.int32)
    crossed = (positions[None, None, None, :] >= bounds[..., None]) & keep_bound[..., None]
    return jnp.sum(crossed.astype(jnp.int32), axis=2).astype(jnp.int32)


def block_scale(own_key, shape, cuts, least, largest):
    def one(dim, blocks):
        steps = jax.random.uniform(jax.random.fold_in(jax.random.fold_in(own_key, 6), dim), (blocks,), jnp.float32, least / len(cuts), largest / len(cuts))
        return jnp.repeat(jnp.exp(steps), shape[dim] // blocks).reshape((-1,) + (1,) * (len(shape) - dim - 1))

    factor_of = one(*cuts[0])
    for cut in cuts[1:]:
        factor_of = factor_of * one(*cut)
    return factor_of


def bell_draw(stream_key, shape, width, most, shards=(), kind=jnp.bfloat16):
    entries = width * jax.random.normal(stream_key, shape, jnp.float32)
    if shards:
        entries = entries * block_scale(stream_key, shape, shards, -0.22, 0.18)
    return jnp.clip(entries, -most, most).astype(kind)


def setup_inputs(seed: int = 0) -> dict:
    streams_of = jax.random.split(jax.random.key(seed), 16)
    return {
        "inputs": bell_draw(streams_of[0], (MICRO, PACKS_ALL, SEQ, D), 1.0, 6.0, ((1, 8), (2, 8))),
        "segments": draw_segments(jax.random.fold_in(streams_of[15], 71), 0),
        "qkv_weight": bell_draw(streams_of[2], (LAYERS, 3, D, D), D ** -0.5, 0.1875, ((0, 2), (3, 8))),
        "qv_bias": bell_draw(streams_of[3], (LAYERS, 2, D), 0.5, 3.0, ((0, 2), (2, 8))),
        "out_weight": bell_draw(streams_of[4], (LAYERS, D, D), (D // 8) ** -0.5, 0.5, ((0, 2), (1, 8))),
        "out_bias": bell_draw(streams_of[5], (LAYERS, D), 0.5, 3.0, ((0, 2),)),
        "gain_one": jnp.clip(1.0 + 0.1 * jax.random.normal(streams_of[6], (LAYERS, D), jnp.float32), 0.5, 1.5).astype(jnp.bfloat16),
        "shift_one": bell_draw(streams_of[7], (LAYERS, D), 0.5, 3.0, ((0, 2),)),
        "up_weight": bell_draw(streams_of[8], (LAYERS, D, FF), D ** -0.5, 0.1875, ((0, 2), (2, 8))),
        "up_bias": bell_draw(streams_of[9], (LAYERS, FF), 0.5, 3.0, ((0, 2), (1, 8))),
        "down_weight": bell_draw(streams_of[10], (LAYERS, FF, D), FF ** -0.5, 0.09375, ((0, 2), (1, 8))),
        "down_bias": bell_draw(streams_of[11], (LAYERS, D), 0.5, 3.0, ((0, 2),)),
        "gain_two": jnp.clip(1.0 + 0.1 * jax.random.normal(streams_of[12], (LAYERS, D), jnp.float32), 0.5, 1.5).astype(jnp.bfloat16),
        "shift_two": bell_draw(streams_of[13], (LAYERS, D), 0.5, 3.0, ((0, 2),)),
        "cotangent": bell_draw(streams_of[14], (MICRO, PACKS_ALL, SEQ, D), 1.0, 6.0, ((1, 8), (2, 8))),
    }


@jax.custom_vjp
def low(v):
    return lax.optimization_barrier(v.astype(jnp.bfloat16)).astype(jnp.float32)

@jax.custom_vjp
def low_back(v):
    return v

def low_keep(v):
    return (low(v), None)

def low_pass(kept, grad):
    return (grad,)

def back_keep(v):
    return (v, None)

def back_low(kept, grad):
    return (low(grad),)
low.defvjp(low_keep, low_pass)
low_back.defvjp(back_keep, back_low)

def layer_norm(values, gain, shift):
    center = values - lax.optimization_barrier(jnp.mean(values, axis=-1, keepdims=True))
    spread = lax.optimization_barrier(jnp.mean(center * center, axis=-1, keepdims=True))
    return center * lax.rsqrt(spread + 1e-06) * gain + shift

def matmul(left, right):
    return jnp.dot(left, right, precision=lax.Precision.HIGHEST, preferred_element_type=jnp.float32)

def attend_pack(operands):
    queries, key_rows, value_rows, seg_ids = operands
    scores = jnp.einsum('qhd,khd->hqk', queries, key_rows, precision=lax.Precision.HIGHEST) * 0.125
    scores = low_back(scores)
    same_doc = seg_ids[:, None] == seg_ids[None, :]
    scores = jnp.where(same_doc[None], scores, -1e+30)
    top_score = lax.optimization_barrier(jnp.max(scores, axis=-1, keepdims=True))
    weights = jnp.exp(scores - top_score)
    probs = low(weights / lax.optimization_barrier(jnp.sum(weights, axis=-1, keepdims=True)))
    return jnp.einsum('hqk,khd->qhd', probs, value_rows, precision=lax.Precision.HIGHEST)

def layer(layer_in, seg_ids, params):
    qkv_w, qv_b, out_w, out_b, gain_a, shift_a, up_w, up_b, down_w, down_b, gain_b, shift_b = params
    token_rows = layer_in.reshape(-1, D)
    queries = low_back(low(matmul(token_rows, qkv_w[0]) + qv_b[0]))
    key_rows = low_back(low(matmul(token_rows, qkv_w[1])))
    value_rows = low_back(low(matmul(token_rows, qkv_w[2]) + qv_b[1]))
    head_shape = (-1, SEQ, HEADS, HEAD_DIM)
    attended = lax.map(jax.checkpoint(attend_pack), (queries.reshape(head_shape), key_rows.reshape(head_shape), value_rows.reshape(head_shape), seg_ids))
    attended = low_back(low(attended.reshape(-1, D)))
    residual = token_rows + low_back(matmul(attended, out_w)) + out_b
    normed = layer_norm(residual, gain_a, shift_a)
    hidden = low_back(matmul(low(normed), up_w)) + up_b
    active = low(jax.nn.gelu(hidden, approximate=False))
    second = normed + low_back(matmul(active, down_w)) + down_b
    return layer_norm(second, gain_b, shift_b).reshape(layer_in.shape)

def reference(inputs, segments, qkv_weight, qv_bias, out_weight, out_bias, gain_one, shift_one, up_weight, up_bias, down_weight, down_bias, gain_two, shift_two, cotangent):
    pack_rows = inputs.reshape(MICRO * PACKS_ALL, SEQ, D).astype(jnp.float32)
    seg_ids = segments.reshape(MICRO * PACKS_ALL, SEQ)
    params = tuple((param.astype(jnp.float32) for param in (qkv_weight, qv_bias, out_weight, out_bias, gain_one, shift_one, up_weight, up_bias, down_weight, down_bias, gain_two, shift_two)))

    def forward(weights, deltas):
        current = pack_rows + deltas[0]
        results = []
        for section_index in range(N_SECTION):
            if section_index > 0:
                current = low_back(low(current) + deltas[section_index])
            current = layer(current, seg_ids, tuple((param[section_index] for param in weights)))
            results.append(current)
        return jnp.stack(results)
    deltas = jnp.zeros((N_SECTION,) + pack_rows.shape, jnp.float32)
    outputs, backward = jax.vjp(forward, params, deltas)
    seeds = jnp.zeros_like(outputs).at[N_SECTION - 1].set(cotangent.reshape(pack_rows.shape).astype(jnp.float32))
    param_grads, delta_grads = backward(seeds)
    full_shape = (N_SECTION, MICRO, PACKS_ALL, SEQ, D)
    return (outputs.reshape(full_shape).astype(jnp.bfloat16), delta_grads.reshape(full_shape).astype(jnp.bfloat16), param_grads[0], param_grads[1], param_grads[2], param_grads[3], param_grads[4], param_grads[5], param_grads[6], param_grads[7], param_grads[8], param_grads[9], param_grads[10], param_grads[11])
```

```python
import jax
import jax.numpy as jnp
from jax import lax
from jax.experimental import pallas as pl
from jax.experimental.pallas import tpu as pltpu
from jax.sharding import Mesh
from jax.sharding import PartitionSpec as P


BF = jnp.bfloat16
F32 = jnp.float32
MESH = pl.DeviceIdType.MESH
D = 1024
FFS = 512
SEQ = 512
BLK = 64
QKV, OUT, UP, DOWN = 0, 1, 2, 3
PIECE = (256, 32, 256, 128)
FA, FM, BM, BA = 0, 1, 2, 3


def remote(src, dst, send, recv, dev):
    return pltpu.make_async_remote_copy(
        src_ref=src, dst_ref=dst, send_sem=send, recv_sem=recv, device_id=dev, device_id_type=MESH
    )


def dot_nn(a, b):
    return lax.dot_general(a, b, (((1,), (0,)), ((), ())), preferred_element_type=F32)


def dot_nt(a, b):
    return lax.dot_general(a, b, (((1,), (1,)), ((), ())), preferred_element_type=F32)


def dot_tn(a, b):
    return lax.dot_general(a, b, (((0,), (0,)), ((), ())), preferred_element_type=F32)


def normed(r):
    center = r - jnp.mean(r, axis=-1, keepdims=True)
    scale = lax.rsqrt(jnp.mean(center * center, axis=-1, keepdims=True) + 1e-06)
    return center * scale, scale


def norm_back(dy, gain, n, scale):
    e = dy * gain
    mean_e = jnp.mean(e, axis=-1, keepdims=True)
    mean_en = jnp.mean(e * n, axis=-1, keepdims=True)
    return (e - mean_e - n * mean_en) * scale


def col_sum(v):
    return jnp.sum(v, axis=0, keepdims=True)


def kernel(
    inp, cot, seg, wq_in, wo_in, wu_in, wd_in, sw_in,
    lo, ig, gq, go, gu, gd, gs,
    wq, wo, wu, wd, sw,
    hbuf, arbuf, dmbuf, dprbuf,
    ain, bin_, aout, bout, part,
    qkv, att, probs, gp, gr, n1, n2, sc1, sc2, abuf, res,
    segb, bias, cotb, dur, dacc, dx,
    yb, lob, dhb, igb, gsb,
    g0, g1, g2, g3,
    zr0, zr1, zr2, zr3,
    yo0, yo1, yo2, yo3,
    yr0, yr1, yr2, yr3,
    f0, f1, f2, f3,
    swap_s, swap_r, wy_s, wy_r, wz_s, wz_r, wl,
    ag_s, ag_r, cg_s, cg_r, ra_s, ra_r, rb_s, rb_r,
    lo_s, lo_r, ig_s, ig_r,
    gz_s, gz_r, gy_s, gy_r, fz_s, fz_r, fc_s, fc_r, st,
):
    s = lax.axis_index("s")
    x = lax.axis_index("x")
    yh = lax.axis_index("yh")
    z = lax.axis_index("z")
    c = lax.axis_index("c")
    diag = c == yh
    weights_in = (wq_in, wo_in, wu_in, wd_in)
    weights = (wq, wo, wu, wd)
    grads = (g0, g1, g2, g3)
    zrecv = (zr0, zr1, zr2, zr3)
    yout = (yo0, yo1, yo2, yo3)
    yrecv = (yr0, yr1, yr2, yr3)
    final = (f0, f1, f2, f3)
    outs = (gq, go, gu, gd)

    def at_piece(ref, k, zi, lead=()):
        rows = pl.ds(pl.multiple_of(zi * PIECE[k], PIECE[k]), PIECE[k])
        if k == QKV:
            return ref.at[(*lead, slice(None), rows)]
        return ref.at[(*lead, rows)]

    def y_dev(i):
        return {"s": lax.rem(s + i % 2, 2), "yh": lax.rem(yh + i // 2, 2)}

    def z_dev(d):
        return {"z": lax.rem(z + d, 4)}

    core = {"c": 1 - c}

    barrier = pltpu.get_barrier_semaphore()

    def greet(dev):
        pl.semaphore_signal(barrier, inc=1, device_id=dev, device_id_type=MESH)

    for d in (1, 2, 3):
        greet({"x": lax.rem(x + d, 4)})
        greet(z_dev(d))
        greet(y_dev(d))
    greet(core)

    @pl.when(diag)
    def _():
        pl.semaphore_wait(barrier, 10)

    @pl.when(jnp.logical_not(diag))
    def _():
        greet({"s": s, "yh": c, "c": yh})
        greet({"s": 1 - s, "yh": c, "c": yh})
        pl.semaphore_wait(barrier, 12)

    own_rows = pl.ds(pl.multiple_of((2 * x + c) * BLK, BLK), BLK)
    mirror = {"yh": c, "c": yh}
    mirror_rows = pl.ds(pl.multiple_of((2 * x + yh) * BLK, BLK), BLK)
    swaps = (
        (inp.at[s], hbuf.at[0, mirror_rows]),
        (seg.at[s], segb),
        (cot.at[s], cotb),
    )

    def swap_start(i):
        src, dst = swaps[i]

        @pl.when(diag)
        def _():
            pltpu.make_async_copy(src, dst, swap_r.at[i]).start()

        @pl.when(jnp.logical_not(diag))
        def _():
            remote(src, dst, swap_s.at[i], swap_r.at[i], mirror).start()

    def swap_wait(i):
        src, dst = swaps[i]

        @pl.when(diag)
        def _():
            pltpu.make_async_copy(src, dst, swap_r.at[i]).wait()

        @pl.when(jnp.logical_not(diag))
        def _():
            remote(src, dst, swap_s.at[i], swap_r.at[i], mirror).wait()

    def wy_copy(k, i):
        if k == 4:
            return remote(sw_in, sw.at[s], wy_s.at[k, i], wy_r.at[s, k], y_dev(i))
        src = at_piece(weights_in[k], k, z)
        return remote(src, at_piece(weights[k], k, z, (s,)), wy_s.at[k, i], wy_r.at[s, k], y_dev(i))

    def wy_arrival(l, k):
        if k == 4:
            return remote(sw_in, sw.at[l], wy_s.at[k, 0], wy_r.at[l, k], core)
        dst = at_piece(weights[k], k, z, (l,))
        return remote(dst, dst, wy_s.at[k, 0], wy_r.at[l, k], core)

    def wl_copy(k):
        if k == 4:
            return pltpu.make_async_copy(sw_in, sw.at[s], wl.at[k])
        return pltpu.make_async_copy(weights_in[k], weights[k].at[s], wl.at[k])

    def wz_copy(l, k, d):
        piece = at_piece(weights[k], k, z, (l,))
        return remote(piece, piece, wz_s.at[l, k, d], wz_r.at[l, k, d], z_dev(d))

    def wz_arrival(l, k, d):
        piece = at_piece(weights[k], k, lax.rem(z + 4 - d, 4), (l,))
        return remote(piece, piece, wz_s.at[l, k, d], wz_r.at[l, k, d], z_dev(d))

    def mine(l):
        return jnp.logical_and(diag, s == l)

    def relay(l, k):
        @pl.when(jnp.logical_not(mine(l)))
        def _():
            wy_arrival(l, k).wait_recv()
            if k != 4:
                for d in (1, 3, 2):
                    wz_copy(l, k, d).start()

    def ready(l, k):
        @pl.when(mine(l))
        def _():
            wl_copy(k).wait()

        @pl.when(jnp.logical_not(mine(l)))
        def _():
            for d in (1, 3, 2):
                wz_arrival(l, k, d).wait_recv()

    def spread(k):
        @pl.when(diag)
        def _():
            for i in (1, 3, 2):
                wy_copy(k, i).start()
            wl_copy(k).start()

    swap_start(0)
    spread(4)
    spread(QKV)
    swap_start(1)
    spread(OUT)
    spread(UP)
    spread(DOWN)
    swap_start(2)

    def arrival(i):
        return i + (i // 2) * (5 - 2 * i)

    def ag_direct(ph, view, d):
        block = view.at[own_rows]
        return remote(block, block, ag_s.at[ph, d], ag_r.at[ph, d], {"x": lax.rem(x + d, 4)})

    def ag_forward(ph, view, d):
        rows = pl.ds(pl.multiple_of((2 * lax.rem(x + 4 - d, 4) + c) * BLK, BLK), BLK)
        block = view.at[rows]
        return remote(block, block, cg_s.at[ph, d], cg_r.at[ph, d], core)

    def ag_start(ph, view):
        for d in (1, 3, 2):
            ag_direct(ph, view, d).start()
        ag_forward(ph, view, 0).start()

    def ag_block(ph, view, i):
        d = arrival(i)

        @pl.when(i > 0)
        def _():
            ag_direct(ph, view, d).wait_recv()
            ag_forward(ph, view, d).start()

        ag_forward(ph, view, d).wait_recv()
        return pl.multiple_of(lax.rem(x + 4 - d, 4) * 128, 128)

    def ag_end(ph, view):
        for d in (1, 2, 3):
            ag_direct(ph, view, d).wait_send()
        for d in range(4):
            ag_forward(ph, view, d).wait_send()

    mine64 = pl.ds(pl.multiple_of(c * BLK, BLK), BLK)
    theirs64 = pl.ds(pl.multiple_of((1 - c) * BLK, BLK), BLK)

    def ra_copy(ph, d):
        return remote(aout.at[d], ain.at[ph, d], ra_s.at[ph, d], ra_r.at[ph, d], core)

    def rb_copy(ph, d):
        return remote(
            bout.at[d], bin_.at[ph, d], rb_s.at[ph, d], rb_r.at[ph, d], {"x": lax.rem(x + 4 - d, 4)}
        )

    def rs_begin(ph, d, value):
        part[d] = value
        aout[d] = part[d, theirs64, :].astype(BF)
        ra_copy(ph, d).start()

    def rs_pass(ph, d):
        ra_copy(ph, d).wait_recv()
        total = part[d, mine64, :] + ain[ph, d].astype(F32)

        @pl.when(d == 0)
        def _():
            res[...] = total

        @pl.when(d != 0)
        def _():
            bout[d] = total.astype(BF)
            rb_copy(ph, d).start()

    def rs_loop(ph, order, step):
        def one(i, carry):
            @pl.when(i < 4)
            def _():
                d = order(i)
                rs_begin(ph, d, step(i, d))

            @pl.when(i > 0)
            def _():
                rs_pass(ph, order(i - 1))

            return carry

        lax.fori_loop(0, 5, one, 0)

    def rs_end(ph):
        total = res[...]
        for d in (1, 3, 2):
            rb_copy(ph, d).wait_recv()
            total = total + bin_[ph, d].astype(F32)
        for d in range(4):
            ra_copy(ph, d).wait_send()
        for d in (1, 2, 3):
            rb_copy(ph, d).wait_send()
        return total

    lanes = lax.broadcasted_iota(jnp.int32, (1, 128), 1) < 64
    head_mask = (
        lanes.astype(F32).astype(BF),
        (1.0 - lanes.astype(F32)).astype(BF),
    )
    first_head = lax.broadcasted_iota(jnp.int32, (128, 128), 1) < 64

    def home_copy(l, src, dst, send, recv):
        return remote(src.at[l], dst.at[s], send.at[l], recv.at[s], {"s": l, "yh": c, "c": yh})

    def home_start(l, src, dst, send, recv):
        @pl.when(mine(l))
        def _():
            dst[s] = src[l]

        @pl.when(jnp.logical_not(mine(l)))
        def _():
            home_copy(l, src, dst, send, recv).start()

    def home_wait(src, dst, send, recv):
        for l in range(2):
            @pl.when(jnp.logical_not(mine(l)))
            def _():
                home_copy(l, src, dst, send, recv).wait_send()
                remote(src.at[l], dst.at[l], send.at[l], recv.at[l], core).wait_recv()

    def reversed_arrival(i):
        return arrival(3 - i)

    swap_wait(0)
    ag_start(FA, hbuf.at[0])
    relay(0, 4)
    relay(0, QKV)
    relay(1, 4)

    @pl.when(diag)
    def _():
        wl_copy(4).wait()

    swap_wait(1)
    documents = lax.broadcasted_iota(jnp.int32, (8, SEQ), 0) == segb[...]
    documents = documents.astype(F32).astype(BF)
    bias[...] = jnp.where(dot_tn(documents, documents) > 0.5, 0.0, -1e30)

    def forward(l, carry):
        small = sw[l]
        out_b, gain_a, shift_a = small[0:1], small[1:2], small[2:3]
        down_b, gain_b, shift_b = small[3:4], small[4:5], small[5:6]
        view = hbuf.at[l]

        @pl.when(l == 1)
        def _():
            ag_start(FA, view)

        ready(l, QKV)

        def project(i, carry):
            r0 = ag_block(FA, view, i)
            rows = hbuf[l, pl.ds(r0, 128), :]
            q = dot_nn(rows, wq[l, 0]) + sw[l, 6:7, 512:640]
            k = dot_nn(rows, wq[l, 1])
            v = dot_nn(rows, wq[l, 2]) + sw[l, 6:7, 640:768]
            qkv[l, 0, pl.ds(r0, 128), :] = q.astype(BF)
            qkv[l, 1, pl.ds(r0, 128), :] = k.astype(BF)
            qkv[l, 2, pl.ds(r0, 128), :] = v.astype(BF)
            return carry

        lax.fori_loop(0, 4, project, 0)

        @pl.when(l == 0)
        def _():
            relay(0, OUT)
            relay(0, UP)

        ready(l, OUT)

        def attend(i, d):
            r0 = pl.multiple_of(lax.rem(x + 4 - d, 4) * 128, 128)
            q = qkv[l, 0, pl.ds(r0, 128), :]
            keys = qkv[l, 1]
            values = qkv[l, 2]
            heads = []
            for h in range(2):
                scores = dot_nt(q * head_mask[h], keys) * 0.125 + bias[pl.ds(r0, 128), :]
                e = jnp.exp(scores - jnp.max(scores, axis=-1, keepdims=True))
                p = (e * (1.0 / jnp.sum(e, axis=-1, keepdims=True))).astype(BF)
                probs[l, h, pl.ds(r0, 128), :] = p
                heads.append(dot_nn(p, values))
            block = jnp.where(first_head, heads[0], heads[1]).astype(BF)
            att[l, pl.ds(r0, 128), :] = block
            return dot_nn(block, wo[l])

        rs_loop(FA, reversed_arrival, attend)

        @pl.when(l == 0)
        def _():
            relay(0, DOWN)
            for k in (QKV, OUT, UP, DOWN):
                relay(1, k)

        r1 = hbuf[l, own_rows, :].astype(F32) + rs_end(FA) + out_b
        ag_end(FA, view)
        n, scale = normed(r1)
        n1[l] = n
        sc1[l] = jnp.broadcast_to(scale, (BLK, 128))
        a = n * gain_a + shift_a
        abuf[...] = a
        arbuf[l, own_rows, :] = a.astype(BF)
        ar_view = arbuf.at[l]
        ag_start(FM, ar_view)
        ready(l, UP)
        ready(l, DOWN)

        def feed(i, d):
            r0 = ag_block(FM, ar_view, i)
            u = dot_nn(arbuf[l, pl.ds(r0, 128), :], wu[l]) + sw[l, 6:7, 0:512]
            cdf = 0.5 * (1.0 + lax.erf(u * 0.7071067811865476))
            gp[l, pl.ds(r0, 128), :] = cdf + u * (jnp.exp(-0.5 * u * u) * 0.3989422804014327)
            g = (u * cdf).astype(BF)
            gr[l, pl.ds(r0, 128), :] = g
            return dot_nn(g, wd[l])

        rs_loop(FM, arrival, feed)
        r2 = abuf[...] + rs_end(FM) + down_b
        ag_end(FM, ar_view)
        n, scale = normed(r2)
        n2[l] = n
        sc2[l] = jnp.broadcast_to(scale, (BLK, 128))
        y = (n * gain_b + shift_b).astype(BF)
        yb[l] = y

        @pl.when(l == 0)
        def _():
            hbuf[1, own_rows, :] = y

        home_start(l, yb, lob, lo_s, lo_r)
        return carry

    lax.fori_loop(0, 2, forward, 0)

    def gz_copy(l, k, d):
        src = at_piece(grads[k], k, lax.rem(z + d, 4), (l,))
        return remote(src, zrecv[k].at[l, d - 1], gz_s.at[l, k, d], gz_r.at[l, k, d], z_dev(d))

    def gz_start(l, k):
        for d in (1, 3, 2):
            gz_copy(l, k, d).start()

    def gy_copy(l, k):
        slot = 2 * lax.rem(yh + 2 - c, 2) + lax.rem(s + 2 - l, 2)
        return remote(
            yout[k].at[l], yrecv[k].at[slot - 1], gy_s.at[l, k], gy_r.at[k, slot], {"s": l, "yh": c}
        )

    def gy_start(l, k):
        total = at_piece(grads[k], k, z, (l,))[...].astype(F32)
        for d in (1, 3, 2):
            gz_copy(l, k, d).wait_recv()
            total = total + zrecv[k][l, d - 1].astype(F32)
        yout[k][l] = total.astype(BF)

        @pl.when(jnp.logical_not(mine(l)))
        def _():
            gy_copy(l, k).start()

    def fz_copy(k, d):
        piece = at_piece(final[k], k, z)
        return remote(piece, piece, fz_s.at[k, d], fz_r.at[k, d], z_dev(d))

    def fc_copy(k, d):
        piece = at_piece(final[k], k, lax.rem(z + 4 - d, 4))
        return remote(piece, piece, fc_s.at[k, d], fc_r.at[k, d], core)

    def fz_start(k):
        @pl.when(diag)
        def _():
            total = yout[k][s].astype(F32)
            for i in (1, 2, 3):
                remote(
                    yrecv[k].at[i - 1], yrecv[k].at[i - 1], gy_s.at[0, k], gy_r.at[k, i], core
                ).wait_recv()
                total = total + yrecv[k][i - 1].astype(F32)
            at_piece(final[k], k, z)[...] = total.astype(BF)
            for d in (1, 3, 2):
                fz_copy(k, d).start()
            fc_copy(k, 0).start()

    def fc_start(k):
        @pl.when(diag)
        def _():
            for d in (1, 3, 2):
                piece = at_piece(final[k], k, lax.rem(z + 4 - d, 4))
                remote(piece, piece, fz_s.at[k, d], fz_r.at[k, d], z_dev(d)).wait_recv()
                fc_copy(k, d).start()

    def out_start(k):
        @pl.when(jnp.logical_not(diag))
        def _():
            for d in range(4):
                fc_copy(k, d).wait_recv()

        pltpu.make_async_copy(final[k], outs[k], st.at[k]).start()

    swap_wait(2)

    def backward(step_index, carry):
        l = 1 - step_index
        small = sw[l]
        gain_a, gain_b = small[1:2], small[4:5]

        @pl.when(l == 1)
        def _():
            res[...] = cotb[...].astype(F32)

        @pl.when(l == 0)
        def _():
            res[...] = dhb[1].astype(F32)

        dy = res[...]
        n = n2[l]
        dr2 = norm_back(dy, gain_b, n, sc2[l, :, 0:1])
        dmbuf[own_rows, :] = dr2.astype(BF)
        ag_start(BM, dmbuf)
        gsb[l] = jnp.zeros((8, D), F32)
        gsb[l, 4:5, :] = col_sum(dy * n)
        gsb[l, 5:6, :] = col_sum(dy)
        gsb[l, 3:4, :] = col_sum(dr2)
        abuf[...] = dr2

        def feed_back(i, d):
            r0 = ag_block(BM, dmbuf, i)
            dg = dot_nt(dmbuf[pl.ds(r0, 128), :], wd[l])
            du = dg * gp[l, pl.ds(r0, 128), :]
            gsb[l, 6:7, 0:512] += col_sum(du)
            low = du.astype(BF)
            dur[pl.ds(r0, 128), :] = low
            return dot_nt(low, wu[l])

        rs_loop(BM, arrival, feed_back)

        def grad_down(i, carry):
            cols = pl.ds(pl.multiple_of(i * 128, 128), 128)
            g3[l, cols, :] = dot_tn(gr[l, :, cols], dmbuf[...]).astype(BF)
            return carry

        lax.fori_loop(0, 4, grad_down, 0)
        gz_start(l, DOWN)

        def grad_up(i, carry):
            cols = pl.ds(pl.multiple_of(i * 128, 128), 128)
            g2[l, cols, :] = dot_tn(arbuf[l, :, cols], dur[...]).astype(BF)
            return carry

        lax.fori_loop(0, 8, grad_up, 0)
        gz_start(l, UP)
        da = abuf[...] + rs_end(BM)
        ag_end(BM, dmbuf)
        n = n1[l]
        dr1 = norm_back(da, gain_a, n, sc1[l, :, 0:1])
        dprbuf[own_rows, :] = dr1.astype(BF)
        ag_start(BA, dprbuf)
        gsb[l, 1:2, :] = col_sum(da * n)
        gsb[l, 2:3, :] = col_sum(da)
        gsb[l, 0:1, :] = col_sum(dr1)
        abuf[...] = dr1
        dacc[...] = jnp.zeros_like(dacc)

        @pl.when(l == 0)
        def _():
            for k in (DOWN, UP):
                gy_start(1, k)

        def attend_back(i, carry):
            r0 = ag_block(BA, dprbuf, i)
            rows = pl.ds(r0, 128)
            grad = dot_nt(dprbuf[rows, :], wo[l]).astype(BF)
            q = qkv[l, 0, rows, :]
            keys = qkv[l, 1]
            values = qkv[l, 2]
            heads = []
            dk = dacc[0]
            dv = dacc[1]
            for h in range(2):
                own = grad * head_mask[h]
                low_p = probs[l, h, rows, :]
                p = low_p.astype(F32)
                dp = dot_nt(own, values)
                ds = (p * (dp - jnp.sum(p * dp, axis=-1, keepdims=True))).astype(BF)
                heads.append(dot_nn(ds, keys))
                dk = dk + dot_tn(ds, q * head_mask[h])
                dv = dv + dot_tn(low_p, own)
            dacc[0] = dk
            dacc[1] = dv
            dq = (jnp.where(first_head, heads[0], heads[1]) * 0.125).astype(BF)
            dx[0, rows, :] = dq
            gsb[l, 6:7, 512:640] += col_sum(dq.astype(F32))
            return carry

        lax.fori_loop(0, 4, attend_back, 0)
        dx[1] = (dacc[0] * 0.125).astype(BF)
        dv = dacc[1].astype(BF)
        dx[2] = dv
        gsb[l, 6:7, 640:768] = col_sum(dv.astype(F32))

        def input_back(i, d):
            rows = pl.ds(pl.multiple_of(lax.rem(x + 4 - d, 4) * 128, 128), 128)
            return (
                dot_nt(dx[0, rows, :], wq[l, 0])
                + dot_nt(dx[1, rows, :], wq[l, 1])
                + dot_nt(dx[2, rows, :], wq[l, 2])
            )

        rs_loop(BA, reversed_arrival, input_back)

        def grad_qkv(i, carry):
            cols = pl.ds(pl.multiple_of(i * 128, 128), 128)
            rows = hbuf[l, :, cols]
            for j in range(3):
                g0[l, j, cols, :] = dot_tn(rows, dx[j]).astype(BF)
            return carry

        lax.fori_loop(0, 8, grad_qkv, 0)
        gz_start(l, QKV)
        g1[l] = dot_tn(att[l], dprbuf[...]).astype(BF)
        gz_start(l, OUT)
        dh = (abuf[...] + rs_end(BA)).astype(BF)
        ag_end(BA, dprbuf)
        dhb[l] = dh
        home_start(l, dhb, igb, ig_s, ig_r)
        return carry

    lax.fori_loop(0, 2, backward, 0)

    small_out = pltpu.make_async_copy(gsb, gs, st.at[4])
    small_out.start()
    for k in (QKV, OUT):
        gy_start(1, k)
    for k in (DOWN, UP):
        gy_start(0, k)
    for k in (DOWN, UP):
        fz_start(k)
    for k in (QKV, OUT):
        gy_start(0, k)
    for k in (DOWN, UP):
        fc_start(k)
    for k in (QKV, OUT):
        fz_start(k)
    home_wait(yb, lob, lo_s, lo_r)
    lo_out = pltpu.make_async_copy(lob, lo, st.at[5])
    lo_out.start()
    home_wait(dhb, igb, ig_s, ig_r)
    ig_out = pltpu.make_async_copy(igb, ig, st.at[6])
    ig_out.start()
    for k in (DOWN, UP):
        out_start(k)
    for k in (QKV, OUT):
        fc_start(k)
    for k in (QKV, OUT):
        out_start(k)

    @pl.when(diag)
    def _():
        for k in range(5):
            for i in (1, 2, 3):
                wy_copy(k, i).wait_send()

    for l in range(2):
        for k in range(4):
            @pl.when(jnp.logical_not(mine(l)))
            def _():
                for d in (1, 2, 3):
                    wz_copy(l, k, d).wait_send()
                gy_copy(l, k).wait_send()

            for d in (1, 2, 3):
                gz_copy(l, k, d).wait_send()

    @pl.when(diag)
    def _():
        for k in range(4):
            for d in (1, 2, 3):
                fz_copy(k, d).wait_send()
            for d in range(4):
                fc_copy(k, d).wait_send()

    small_out.wait()
    lo_out.wait()
    ig_out.wait()
    for k in range(4):
        pltpu.make_async_copy(final[k], outs[k], st.at[k]).wait()


WSHAPES = ((3, D, 128), (128, D), (D, FFS), (FFS, D))
PSHAPES = ((3, 256, 128), (32, D), (256, FFS), (128, D))


def run(inp, cot, seg, wq, wo, wu, wd, sw):
    vm = pltpu.VMEM
    scratch = [vm((2, *shape), BF) for shape in WSHAPES]
    scratch += [vm((2, 8, D), F32)]
    scratch += [vm((2, SEQ, D), BF)] * 2 + [vm((SEQ, D), BF)] * 2
    scratch += [vm((4, 4, BLK, D), BF)] * 2 + [vm((4, BLK, D), BF)] * 2 + [vm((4, 128, D), F32)]
    scratch += [
        vm((2, 3, SEQ, 128), BF),
        vm((2, SEQ, 128), BF),
        vm((2, 2, SEQ, SEQ), BF),
        vm((2, SEQ, FFS), F32),
        vm((2, SEQ, FFS), BF),
        vm((2, BLK, D), F32),
        vm((2, BLK, D), F32),
        vm((2, BLK, 128), F32),
        vm((2, BLK, 128), F32),
        vm((BLK, D), F32),
        vm((BLK, D), F32),
    ]
    scratch += [
        vm((8, SEQ), jnp.int32),
        vm((SEQ, SEQ), F32),
        vm((BLK, D), BF),
        vm((SEQ, FFS), BF),
        vm((2, SEQ, 128), F32),
        vm((3, SEQ, 128), BF),
    ]
    scratch += [vm((2, BLK, D), BF)] * 4 + [vm((2, 8, D), F32)]
    scratch += [vm((2, *shape), BF) for shape in WSHAPES]
    scratch += [vm((2, 3, *shape), BF) for shape in PSHAPES]
    scratch += [vm((2, *shape), BF) for shape in PSHAPES]
    scratch += [vm((3, *shape), BF) for shape in PSHAPES]
    scratch += [vm(shape, BF) for shape in WSHAPES]
    dma = pltpu.SemaphoreType.DMA
    scratch += [dma((3,)), dma((3,)), dma((5, 4)), dma((2, 5)), dma((2, 4, 4)), dma((2, 4, 4)), dma((5,))]
    scratch += [dma((4, 4))] * 8
    scratch += [dma((2,))] * 4
    scratch += [dma((2, 4, 4)), dma((2, 4, 4)), dma((2, 4)), dma((4, 4))]
    scratch += [dma((4, 4))] * 4 + [dma((7,))]
    any_space = pl.BlockSpec(memory_space=pl.ANY)
    return pl.pallas_call(
        kernel,
        out_shape=[
            jax.ShapeDtypeStruct((2, BLK, D), BF),
            jax.ShapeDtypeStruct((2, BLK, D), BF),
            *(jax.ShapeDtypeStruct(shape, BF) for shape in WSHAPES),
            jax.ShapeDtypeStruct((2, 8, D), F32),
        ],
        in_specs=[any_space] * 8,
        out_specs=[any_space] * 7,
        scratch_shapes=scratch,
        compiler_params=pltpu.CompilerParams(
            collective_id=0, has_side_effects=True, vmem_limit_bytes=60 * 1024 * 1024
        ),
    )(inp, cot, seg, wq, wo, wu, wd, sw)


def local(
    inputs, segments, qkv_weight, qv_bias, out_weight, out_bias, gain_one, shift_one,
    up_weight, up_bias, down_weight, down_bias, gain_two, shift_two, cotangent,
):
    x = lax.axis_index("x")
    yh = lax.axis_index("yh")
    s = lax.axis_index("s")
    c = lax.axis_index("c")
    mixed = jnp.concatenate(
        [up_bias.astype(F32), qv_bias.reshape(1, 256).astype(F32), jnp.zeros((1, 256), F32)], axis=1
    )
    small = jnp.concatenate(
        [v.astype(F32) for v in (out_bias, gain_one, shift_one, down_bias, gain_two, shift_two)]
        + [mixed, jnp.zeros((1, D), F32)],
        axis=0,
    )
    seg = jnp.broadcast_to(segments, (2, 8, SEQ))
    lo, ig, gq, go, gu, gd, gs = run(
        inputs[:, 0], cotangent[:, 0], seg,
        qkv_weight[0], out_weight[0], up_weight[0], down_weight[0], small,
    )
    slot = (lax.broadcasted_iota(jnp.int32, (8, 1, 1), 0) == 2 * x + c).astype(F32)
    mixed_sums = slot * gs[None, :, 6, :768]
    wide, mixed_sums = lax.psum((gs[:, :6], mixed_sums), ("s", "x", "yh", "z", "c"))
    wide = lax.dynamic_index_in_dim(wide, s, 0, keepdims=False)
    mixed_sums = lax.dynamic_index_in_dim(mixed_sums, 2 * x + yh, 0, keepdims=False)
    mixed_sums = lax.dynamic_index_in_dim(mixed_sums, s, 0, keepdims=True)
    return (
        lo[None, :, None],
        ig[None, :, None],
        gq[None].astype(F32),
        mixed_sums[:, 512:768].reshape(1, 2, 128),
        go[None].astype(F32),
        wide[0:1],
        wide[1:2],
        wide[2:3],
        gu[None].astype(F32),
        mixed_sums[:, 0:512],
        gd[None].astype(F32),
        wide[3:4],
        wide[4:5],
        wide[5:6],
    )


def solution(mesh):
    fine = Mesh(mesh.devices.reshape(2, 4, 2, 4, 2), ("s", "x", "yh", "z", "c"))
    t = ("x", "yh")
    dp = ("z", "c")
    return jax.shard_map(
        local,
        mesh=fine,
        in_specs=(
            P(None, dp, t, None),
            P(None, dp, None),
            P("s", None, None, t),
            P("s", None, t),
            P("s", t, None),
            P("s", None),
            P("s", None),
            P("s", None),
            P("s", None, t),
            P("s", t),
            P("s", t, None),
            P("s", None),
            P("s", None),
            P("s", None),
            P(None, dp, t, None),
        ),
        out_specs=(
            P("s", None, dp, t, None),
            P("s", None, dp, t, None),
            P("s", None, None, t),
            P("s", None, t),
            P("s", t, None),
            P("s", None),
            P("s", None),
            P("s", None),
            P("s", None, t),
            P("s", t),
            P("s", t, None),
            P("s", None),
            P("s", None),
            P("s", None),
        ),
        check_vma=False,
    )
```

```python
import jax
import jax.numpy as jnp
from jax import lax
from jax.experimental import pallas as pl
from jax.experimental.pallas import tpu as pltpu
from jax.sharding import Mesh
from jax.sharding import PartitionSpec as P


BF = jnp.bfloat16
F32 = jnp.float32
MESH = pl.DeviceIdType.MESH
D = 1024
FFS = 512
SEQ = 512
BLK = 64
QKV, OUT, UP, DOWN = 0, 1, 2, 3
PIECE = (256, 32, 256, 128)
FA, FM, BM, BA = 0, 1, 2, 3


def remote(src, dst, send, recv, dev):
    return pltpu.make_async_remote_copy(
        src_ref=src, dst_ref=dst, send_sem=send, recv_sem=recv, device_id=dev, device_id_type=MESH
    )


def dot_nn(a, b):
    return lax.dot_general(a, b, (((1,), (0,)), ((), ())), preferred_element_type=F32)


def dot_nt(a, b):
    return lax.dot_general(a, b, (((1,), (1,)), ((), ())), preferred_element_type=F32)


def dot_tn(a, b):
    return lax.dot_general(a, b, (((0,), (0,)), ((), ())), preferred_element_type=F32)


def normed(r):
    center = r - jnp.mean(r, axis=-1, keepdims=True)
    scale = lax.rsqrt(jnp.mean(center * center, axis=-1, keepdims=True) + 1e-06)
    return center * scale, scale


def norm_back(dy, gain, n, scale):
    e = dy * gain
    mean_e = jnp.mean(e, axis=-1, keepdims=True)
    mean_en = jnp.mean(e * n, axis=-1, keepdims=True)
    return (e - mean_e - n * mean_en) * scale


def col_sum(v):
    return jnp.sum(v, axis=0, keepdims=True)


def kernel(
    inp, cot, seg_in, wq_in, wo_in, wu_in, wd_in,
    ob_in, ga_in, sa_in, db_in, gb_in, sb_in, ub_in, qb_in,
    lo, ig, gq, go, gu, gd, gs,
    sw_in, seg,
    wq, wo, wu, wd, sw,
    hbuf, arbuf, dmbuf, dprbuf,
    ain, bin_, aout, bout, part,
    qkv, att, probs, gp, gr, n1, n2, sc1, sc2, abuf, res,
    segb, bias, cotb, dur, dacc, dx,
    yb, lob, dhb, igb, gsb, sx, sc, sz, sy, gsout,
    g0, g1, g2, g3,
    zr0, zr1, zr2, zr3,
    yo0, yo1, yo2, yo3,
    yr0, yr1, yr2, yr3,
    f0, f1, f2, f3,
    swap_s, swap_r, wy_s, wy_r, wz_s, wz_r, wl,
    ag_s, ag_r, cg_s, cg_r, ra_s, ra_r, rb_s, rb_r,
    lo_s, lo_r, ig_s, ig_r,
    gz_s, gz_r, gy_s, gy_r, fz_s, fz_r, fc_s, fc_r, st, sx_s, sx_r, sc_s, sc_r, sz_s, sz_r, sy_s, sy_r,
):
    s = lax.axis_index("s")
    x = lax.axis_index("x")
    yh = lax.axis_index("yh")
    z = lax.axis_index("z")
    c = lax.axis_index("c")
    diag = c == yh
    weights_in = (wq_in, wo_in, wu_in, wd_in)
    weights = (wq, wo, wu, wd)
    grads = (g0, g1, g2, g3)
    zrecv = (zr0, zr1, zr2, zr3)
    yout = (yo0, yo1, yo2, yo3)
    yrecv = (yr0, yr1, yr2, yr3)
    final = (f0, f1, f2, f3)
    outs = (gq, go, gu, gd)

    def at_piece(ref, k, zi, lead=()):
        rows = pl.ds(pl.multiple_of(zi * PIECE[k], PIECE[k]), PIECE[k])
        if k == QKV:
            return ref.at[(*lead, slice(None), rows)]
        return ref.at[(*lead, rows)]

    def y_dev(i):
        return {"s": lax.rem(s + i % 2, 2), "yh": lax.rem(yh + i // 2, 2)}

    def z_dev(d):
        return {"z": lax.rem(z + d, 4)}

    core = {"c": 1 - c}

    for i, ref in enumerate((ob_in, ga_in, sa_in, db_in, gb_in, sb_in)):
        sw_in[i : i + 1, :] = ref[...].astype(F32)
    sw_in[6:7, 0:512] = ub_in[...].astype(F32)
    sw_in[6:7, 512:640] = qb_in[0, 0:1, :].astype(F32)
    sw_in[6:7, 640:768] = qb_in[0, 1:2, :].astype(F32)
    for m in range(2):
        seg[m] = jnp.broadcast_to(seg_in[m], (8, SEQ))

    barrier = pltpu.get_barrier_semaphore()

    def greet(dev):
        pl.semaphore_signal(barrier, inc=1, device_id=dev, device_id_type=MESH)

    for d in (1, 2, 3):
        greet({"x": lax.rem(x + d, 4)})
        greet(z_dev(d))
        greet(y_dev(d))
    greet(core)

    @pl.when(diag)
    def _():
        pl.semaphore_wait(barrier, 10)

    @pl.when(jnp.logical_not(diag))
    def _():
        greet({"s": s, "yh": c, "c": yh})
        greet({"s": 1 - s, "yh": c, "c": yh})
        pl.semaphore_wait(barrier, 12)

    own_rows = pl.ds(pl.multiple_of((2 * x + c) * BLK, BLK), BLK)
    mirror = {"yh": c, "c": yh}
    mirror_rows = pl.ds(pl.multiple_of((2 * x + yh) * BLK, BLK), BLK)
    swaps = (
        (inp.at[s], hbuf.at[0, mirror_rows]),
        (seg.at[s], segb),
        (cot.at[s], cotb),
    )

    def swap_start(i):
        src, dst = swaps[i]

        @pl.when(diag)
        def _():
            pltpu.make_async_copy(src, dst, swap_r.at[i]).start()

        @pl.when(jnp.logical_not(diag))
        def _():
            remote(src, dst, swap_s.at[i], swap_r.at[i], mirror).start()

    def swap_wait(i):
        src, dst = swaps[i]

        @pl.when(diag)
        def _():
            pltpu.make_async_copy(src, dst, swap_r.at[i]).wait()

        @pl.when(jnp.logical_not(diag))
        def _():
            remote(src, dst, swap_s.at[i], swap_r.at[i], mirror).wait()

    def wy_copy(k, i):
        if k == 4:
            return remote(sw_in, sw.at[s], wy_s.at[k, i], wy_r.at[s, k], y_dev(i))
        src = at_piece(weights_in[k], k, z)
        return remote(src, at_piece(weights[k], k, z, (s,)), wy_s.at[k, i], wy_r.at[s, k], y_dev(i))

    def wy_arrival(l, k):
        if k == 4:
            return remote(sw_in, sw.at[l], wy_s.at[k, 0], wy_r.at[l, k], core)
        dst = at_piece(weights[k], k, z, (l,))
        return remote(dst, dst, wy_s.at[k, 0], wy_r.at[l, k], core)

    def wl_copy(k):
        if k == 4:
            return pltpu.make_async_copy(sw_in, sw.at[s], wl.at[k])
        return pltpu.make_async_copy(weights_in[k], weights[k].at[s], wl.at[k])

    def wz_copy(l, k, d):
        piece = at_piece(weights[k], k, z, (l,))
        return remote(piece, piece, wz_s.at[l, k, d], wz_r.at[l, k, d], z_dev(d))

    def wz_arrival(l, k, d):
        piece = at_piece(weights[k], k, lax.rem(z + 4 - d, 4), (l,))
        return remote(piece, piece, wz_s.at[l, k, d], wz_r.at[l, k, d], z_dev(d))

    def mine(l):
        return jnp.logical_and(diag, s == l)

    def relay(l, k):
        @pl.when(jnp.logical_not(mine(l)))
        def _():
            wy_arrival(l, k).wait_recv()
            if k != 4:
                for d in (1, 3, 2):
                    wz_copy(l, k, d).start()

    def ready(l, k):
        @pl.when(mine(l))
        def _():
            wl_copy(k).wait()

        @pl.when(jnp.logical_not(mine(l)))
        def _():
            for d in (1, 3, 2):
                wz_arrival(l, k, d).wait_recv()

    def spread(k):
        @pl.when(diag)
        def _():
            for i in (1, 3, 2):
                wy_copy(k, i).start()
            wl_copy(k).start()

    swap_start(0)
    spread(4)
    spread(QKV)
    swap_start(1)
    spread(OUT)
    spread(UP)
    spread(DOWN)
    swap_start(2)

    def arrival(i):
        return i + (i // 2) * (5 - 2 * i)

    def ag_direct(ph, view, d):
        block = view.at[own_rows]
        return remote(block, block, ag_s.at[ph, d], ag_r.at[ph, d], {"x": lax.rem(x + d, 4)})

    def ag_forward(ph, view, d):
        rows = pl.ds(pl.multiple_of((2 * lax.rem(x + 4 - d, 4) + c) * BLK, BLK), BLK)
        block = view.at[rows]
        return remote(block, block, cg_s.at[ph, d], cg_r.at[ph, d], core)

    def ag_start(ph, view):
        for d in (1, 3, 2):
            ag_direct(ph, view, d).start()
        ag_forward(ph, view, 0).start()

    def ag_block(ph, view, i):
        d = arrival(i)

        @pl.when(i > 0)
        def _():
            ag_direct(ph, view, d).wait_recv()
            ag_forward(ph, view, d).start()

        ag_forward(ph, view, d).wait_recv()
        return pl.multiple_of(lax.rem(x + 4 - d, 4) * 128, 128)

    def ag_end(ph, view):
        for d in (1, 2, 3):
            ag_direct(ph, view, d).wait_send()
        for d in range(4):
            ag_forward(ph, view, d).wait_send()

    mine64 = pl.ds(pl.multiple_of(c * BLK, BLK), BLK)
    theirs64 = pl.ds(pl.multiple_of((1 - c) * BLK, BLK), BLK)

    def ra_copy(ph, d):
        return remote(aout.at[d], ain.at[ph, d], ra_s.at[ph, d], ra_r.at[ph, d], core)

    def rb_copy(ph, d):
        return remote(
            bout.at[d], bin_.at[ph, d], rb_s.at[ph, d], rb_r.at[ph, d], {"x": lax.rem(x + 4 - d, 4)}
        )

    def rs_begin(ph, d, value):
        part[d] = value
        aout[d] = part[d, theirs64, :].astype(BF)
        ra_copy(ph, d).start()

    def rs_pass(ph, d):
        ra_copy(ph, d).wait_recv()
        total = part[d, mine64, :] + ain[ph, d].astype(F32)

        @pl.when(d == 0)
        def _():
            res[...] = total

        @pl.when(d != 0)
        def _():
            bout[d] = total.astype(BF)
            rb_copy(ph, d).start()

    def rs_loop(ph, order, step):
        def one(i, carry):
            @pl.when(i < 4)
            def _():
                d = order(i)
                rs_begin(ph, d, step(i, d))

            @pl.when(i > 0)
            def _():
                rs_pass(ph, order(i - 1))

            return carry

        lax.fori_loop(0, 5, one, 0)

    def rs_end(ph):
        total = res[...]
        for d in (1, 3, 2):
            rb_copy(ph, d).wait_recv()
            total = total + bin_[ph, d].astype(F32)
        for d in range(4):
            ra_copy(ph, d).wait_send()
        for d in (1, 2, 3):
            rb_copy(ph, d).wait_send()
        return total

    lanes = lax.broadcasted_iota(jnp.int32, (1, 128), 1) < 64
    head_mask = (
        lanes.astype(F32).astype(BF),
        (1.0 - lanes.astype(F32)).astype(BF),
    )
    first_head = lax.broadcasted_iota(jnp.int32, (128, 128), 1) < 64

    def home_copy(l, src, dst, send, recv):
        return remote(src.at[l], dst.at[s], send.at[l], recv.at[s], {"s": l, "yh": c, "c": yh})

    def home_start(l, src, dst, send, recv):
        @pl.when(mine(l))
        def _():
            dst[s] = src[l]

        @pl.when(jnp.logical_not(mine(l)))
        def _():
            home_copy(l, src, dst, send, recv).start()

    def home_wait(src, dst, send, recv):
        for l in range(2):
            @pl.when(jnp.logical_not(mine(l)))
            def _():
                home_copy(l, src, dst, send, recv).wait_send()
                remote(src.at[l], dst.at[l], send.at[l], recv.at[l], core).wait_recv()

    def reversed_arrival(i):
        return arrival(3 - i)

    swap_wait(0)
    ag_start(FA, hbuf.at[0])
    relay(0, 4)
    relay(0, QKV)
    relay(1, 4)

    @pl.when(diag)
    def _():
        wl_copy(4).wait()

    swap_wait(1)
    documents = lax.broadcasted_iota(jnp.int32, (8, SEQ), 0) == segb[...]
    documents = documents.astype(F32).astype(BF)
    bias[...] = jnp.where(dot_tn(documents, documents) > 0.5, 0.0, -1e30)

    def forward(l, carry):
        small = sw[l]
        out_b, gain_a, shift_a = small[0:1], small[1:2], small[2:3]
        down_b, gain_b, shift_b = small[3:4], small[4:5], small[5:6]
        view = hbuf.at[l]

        @pl.when(l == 1)
        def _():
            ag_start(FA, view)

        ready(l, QKV)

        def project(i, carry):
            r0 = ag_block(FA, view, i)
            rows = hbuf[l, pl.ds(r0, 128), :]
            q = dot_nn(rows, wq[l, 0]) + sw[l, 6:7, 512:640]
            k = dot_nn(rows, wq[l, 1])
            v = dot_nn(rows, wq[l, 2]) + sw[l, 6:7, 640:768]
            qkv[l, 0, pl.ds(r0, 128), :] = q.astype(BF)
            qkv[l, 1, pl.ds(r0, 128), :] = k.astype(BF)
            qkv[l, 2, pl.ds(r0, 128), :] = v.astype(BF)
            return carry

        lax.fori_loop(0, 4, project, 0)

        @pl.when(l == 0)
        def _():
            relay(0, OUT)
            relay(0, UP)

        ready(l, OUT)

        def attend(i, d):
            r0 = pl.multiple_of(lax.rem(x + 4 - d, 4) * 128, 128)
            q = qkv[l, 0, pl.ds(r0, 128), :]
            keys = qkv[l, 1]
            values = qkv[l, 2]
            heads = []
            for h in range(2):
                scores = dot_nt(q * head_mask[h], keys) * 0.125 + bias[pl.ds(r0, 128), :]
                e = jnp.exp(scores - jnp.max(scores, axis=-1, keepdims=True))
                p = (e * (1.0 / jnp.sum(e, axis=-1, keepdims=True))).astype(BF)
                probs[l, h, pl.ds(r0, 128), :] = p
                heads.append(dot_nn(p, values))
            block = jnp.where(first_head, heads[0], heads[1]).astype(BF)
            att[l, pl.ds(r0, 128), :] = block
            return dot_nn(block, wo[l])

        rs_loop(FA, reversed_arrival, attend)

        @pl.when(l == 0)
        def _():
            relay(0, DOWN)
            for k in (QKV, OUT, UP, DOWN):
                relay(1, k)

        r1 = hbuf[l, own_rows, :].astype(F32) + rs_end(FA) + out_b
        ag_end(FA, view)
        n, scale = normed(r1)
        n1[l] = n
        sc1[l] = jnp.broadcast_to(scale, (BLK, 128))
        a = n * gain_a + shift_a
        abuf[...] = a
        arbuf[l, own_rows, :] = a.astype(BF)
        ar_view = arbuf.at[l]
        ag_start(FM, ar_view)
        ready(l, UP)
        ready(l, DOWN)

        def feed(i, d):
            r0 = ag_block(FM, ar_view, i)
            u = dot_nn(arbuf[l, pl.ds(r0, 128), :], wu[l]) + sw[l, 6:7, 0:512]
            cdf = 0.5 * (1.0 + lax.erf(u * 0.7071067811865476))
            gp[l, pl.ds(r0, 128), :] = cdf + u * (jnp.exp(-0.5 * u * u) * 0.3989422804014327)
            g = (u * cdf).astype(BF)
            gr[l, pl.ds(r0, 128), :] = g
            return dot_nn(g, wd[l])

        rs_loop(FM, arrival, feed)
        r2 = abuf[...] + rs_end(FM) + down_b
        ag_end(FM, ar_view)
        n, scale = normed(r2)
        n2[l] = n
        sc2[l] = jnp.broadcast_to(scale, (BLK, 128))
        y = (n * gain_b + shift_b).astype(BF)
        yb[l] = y

        @pl.when(l == 0)
        def _():
            hbuf[1, own_rows, :] = y

        home_start(l, yb, lob, lo_s, lo_r)
        return carry

    lax.fori_loop(0, 2, forward, 0)

    def gz_copy(l, k, d):
        src = at_piece(grads[k], k, lax.rem(z + d, 4), (l,))
        return remote(src, zrecv[k].at[l, d - 1], gz_s.at[l, k, d], gz_r.at[l, k, d], z_dev(d))

    def gz_start(l, k):
        for d in (1, 3, 2):
            gz_copy(l, k, d).start()

    def gy_copy(l, k):
        slot = 2 * lax.rem(yh + 2 - c, 2) + lax.rem(s + 2 - l, 2)
        return remote(
            yout[k].at[l], yrecv[k].at[slot - 1], gy_s.at[l, k], gy_r.at[k, slot], {"s": l, "yh": c}
        )

    def gy_start(l, k):
        total = at_piece(grads[k], k, z, (l,))[...].astype(F32)
        for d in (1, 3, 2):
            gz_copy(l, k, d).wait_recv()
            total = total + zrecv[k][l, d - 1].astype(F32)
        yout[k][l] = total.astype(BF)

        @pl.when(jnp.logical_not(mine(l)))
        def _():
            gy_copy(l, k).start()

    def fz_copy(k, d):
        piece = at_piece(final[k], k, z)
        return remote(piece, piece, fz_s.at[k, d], fz_r.at[k, d], z_dev(d))

    def fc_copy(k, d):
        piece = at_piece(final[k], k, lax.rem(z + 4 - d, 4))
        return remote(piece, piece, fc_s.at[k, d], fc_r.at[k, d], core)

    def fz_start(k):
        @pl.when(diag)
        def _():
            total = yout[k][s].astype(F32)
            for i in (1, 2, 3):
                remote(
                    yrecv[k].at[i - 1], yrecv[k].at[i - 1], gy_s.at[0, k], gy_r.at[k, i], core
                ).wait_recv()
                total = total + yrecv[k][i - 1].astype(F32)
            at_piece(final[k], k, z)[...] = total.astype(BF)
            for d in (1, 3, 2):
                fz_copy(k, d).start()
            fc_copy(k, 0).start()

    def fc_start(k):
        @pl.when(diag)
        def _():
            for d in (1, 3, 2):
                piece = at_piece(final[k], k, lax.rem(z + 4 - d, 4))
                remote(piece, piece, fz_s.at[k, d], fz_r.at[k, d], z_dev(d)).wait_recv()
                fc_copy(k, d).start()

    def out_start(k):
        @pl.when(jnp.logical_not(diag))
        def _():
            for d in range(4):
                fc_copy(k, d).wait_recv()

        pltpu.make_async_copy(final[k], outs[k], st.at[k]).start()

    def sx_copy(l, d):
        return remote(gsb.at[l], sx.at[l, x], sx_s.at[l, d], sx_r.at[l, d], {"x": lax.rem(x + d, 4)})

    def sc_copy(l):
        return remote(sc.at[l, c], sc.at[l, c], sc_s.at[l], sc_r.at[l], core)

    def sz_copy(l, d):
        return remote(sz.at[l, z], sz.at[l, z], sz_s.at[l, d], sz_r.at[l, d], z_dev(d))

    def sy_copy(l, i):
        block = sy.at[l, 2 * yh + s]
        return remote(block, block, sy_s.at[l, i], sy_r.at[l, i], y_dev(i))

    def small_x(l):
        sx[l, x] = gsb[l]
        for d in (1, 3, 2):
            sx_copy(l, d).start()

    def small_core(l):
        for d in (1, 3, 2):
            sx_copy(l, d).wait_recv()
        sc[l, c] = ((sx[l, 0] + sx[l, 1]) + sx[l, 2]) + sx[l, 3]
        sc[l, c, 6:7, :] = gsb[l, 6:7, :]
        sc_copy(l).start()

    def small_z(l):
        sc_copy(l).wait_recv()
        sz[l, z] = sc[l, 0] + sc[l, 1]
        sz[l, z, 6:7, :] = sc[l, 0, 6:7, :]
        sz[l, z, 7:8, :] = sc[l, 1, 6:7, :]
        for d in (1, 3, 2):
            sz_copy(l, d).start()

    def small_y(l):
        for d in (1, 3, 2):
            sz_copy(l, d).wait_recv()
        sy[l, 2 * yh + s] = ((sz[l, 0] + sz[l, 1]) + sz[l, 2]) + sz[l, 3]
        for i in (1, 3, 2):
            sy_copy(l, i).start()

    def small_end():
        for l in range(2):
            for i in (1, 3, 2):
                sy_copy(l, i).wait_recv()
        gsout[...] = ((sy[s, 0] + sy[s, 1]) + sy[s, 2]) + sy[s, 3]

        @pl.when(yh == 1)
        def _():
            gsout[6:7, :] = gsout[7:8, :]

    swap_wait(2)

    def backward(step_index, carry):
        l = 1 - step_index
        small = sw[l]
        gain_a, gain_b = small[1:2], small[4:5]

        @pl.when(l == 1)
        def _():
            res[...] = cotb[...].astype(F32)

        @pl.when(l == 0)
        def _():
            res[...] = dhb[1].astype(F32)

        dy = res[...]
        n = n2[l]
        dr2 = norm_back(dy, gain_b, n, sc2[l, :, 0:1])
        dmbuf[own_rows, :] = dr2.astype(BF)
        ag_start(BM, dmbuf)
        gsb[l] = jnp.zeros((8, D), F32)
        gsb[l, 4:5, :] = col_sum(dy * n)
        gsb[l, 5:6, :] = col_sum(dy)
        gsb[l, 3:4, :] = col_sum(dr2)
        abuf[...] = dr2

        def feed_back(i, d):
            r0 = ag_block(BM, dmbuf, i)
            dg = dot_nt(dmbuf[pl.ds(r0, 128), :], wd[l])
            du = dg * gp[l, pl.ds(r0, 128), :]
            gsb[l, 6:7, 0:512] += col_sum(du)
            low = du.astype(BF)
            dur[pl.ds(r0, 128), :] = low
            return dot_nt(low, wu[l])

        rs_loop(BM, arrival, feed_back)

        def grad_down(i, carry):
            cols = pl.ds(pl.multiple_of(i * 128, 128), 128)
            g3[l, cols, :] = dot_tn(gr[l, :, cols], dmbuf[...]).astype(BF)
            return carry

        lax.fori_loop(0, 4, grad_down, 0)
        gz_start(l, DOWN)

        def grad_up(i, carry):
            cols = pl.ds(pl.multiple_of(i * 128, 128), 128)
            g2[l, cols, :] = dot_tn(arbuf[l, :, cols], dur[...]).astype(BF)
            return carry

        lax.fori_loop(0, 8, grad_up, 0)
        gz_start(l, UP)
        da = abuf[...] + rs_end(BM)
        ag_end(BM, dmbuf)
        n = n1[l]
        dr1 = norm_back(da, gain_a, n, sc1[l, :, 0:1])
        dprbuf[own_rows, :] = dr1.astype(BF)
        ag_start(BA, dprbuf)
        gsb[l, 1:2, :] = col_sum(da * n)
        gsb[l, 2:3, :] = col_sum(da)
        gsb[l, 0:1, :] = col_sum(dr1)
        abuf[...] = dr1
        dacc[...] = jnp.zeros_like(dacc)

        @pl.when(l == 0)
        def _():
            for k in (DOWN, UP):
                gy_start(1, k)

        def attend_back(i, carry):
            r0 = ag_block(BA, dprbuf, i)
            rows = pl.ds(r0, 128)
            grad = dot_nt(dprbuf[rows, :], wo[l]).astype(BF)
            q = qkv[l, 0, rows, :]
            keys = qkv[l, 1]
            values = qkv[l, 2]
            heads = []
            dk = dacc[0]
            dv = dacc[1]
            for h in range(2):
                own = grad * head_mask[h]
                low_p = probs[l, h, rows, :]
                p = low_p.astype(F32)
                dp = dot_nt(own, values)
                ds = (p * (dp - jnp.sum(p * dp, axis=-1, keepdims=True))).astype(BF)
                heads.append(dot_nn(ds, keys))
                dk = dk + dot_tn(ds, q * head_mask[h])
                dv = dv + dot_tn(low_p, own)
            dacc[0] = dk
            dacc[1] = dv
            dq = (jnp.where(first_head, heads[0], heads[1]) * 0.125).astype(BF)
            dx[0, rows, :] = dq
            gsb[l, 6:7, 512:640] += col_sum(dq.astype(F32))
            return carry

        lax.fori_loop(0, 4, attend_back, 0)
        dx[1] = (dacc[0] * 0.125).astype(BF)
        dv = dacc[1].astype(BF)
        dx[2] = dv
        gsb[l, 6:7, 640:768] = col_sum(dv.astype(F32))
        small_x(l)

        def input_back(i, d):
            rows = pl.ds(pl.multiple_of(lax.rem(x + 4 - d, 4) * 128, 128), 128)
            return (
                dot_nt(dx[0, rows, :], wq[l, 0])
                + dot_nt(dx[1, rows, :], wq[l, 1])
                + dot_nt(dx[2, rows, :], wq[l, 2])
            )

        rs_loop(BA, reversed_arrival, input_back)
        small_core(l)

        def grad_qkv(i, carry):
            cols = pl.ds(pl.multiple_of(i * 128, 128), 128)
            rows = hbuf[l, :, cols]
            for j in range(3):
                g0[l, j, cols, :] = dot_tn(rows, dx[j]).astype(BF)
            return carry

        lax.fori_loop(0, 8, grad_qkv, 0)
        gz_start(l, QKV)
        g1[l] = dot_tn(att[l], dprbuf[...]).astype(BF)
        gz_start(l, OUT)
        small_z(l)
        dh = (abuf[...] + rs_end(BA)).astype(BF)
        ag_end(BA, dprbuf)
        dhb[l] = dh
        home_start(l, dhb, igb, ig_s, ig_r)
        small_y(l)
        return carry

    lax.fori_loop(0, 2, backward, 0)

    for k in (QKV, OUT):
        gy_start(1, k)
    for k in (DOWN, UP):
        gy_start(0, k)
    for k in (DOWN, UP):
        fz_start(k)
    for k in (QKV, OUT):
        gy_start(0, k)
    for k in (DOWN, UP):
        fc_start(k)
    for k in (QKV, OUT):
        fz_start(k)
    home_wait(yb, lob, lo_s, lo_r)
    lo_out = pltpu.make_async_copy(lob, lo, st.at[5])
    lo_out.start()
    home_wait(dhb, igb, ig_s, ig_r)
    ig_out = pltpu.make_async_copy(igb, ig, st.at[6])
    ig_out.start()
    small_end()
    small_out = pltpu.make_async_copy(gsout, gs, st.at[4])
    small_out.start()
    for k in (DOWN, UP):
        out_start(k)
    for k in (QKV, OUT):
        fc_start(k)
    for k in (QKV, OUT):
        out_start(k)

    @pl.when(diag)
    def _():
        for k in range(5):
            for i in (1, 2, 3):
                wy_copy(k, i).wait_send()

    for l in range(2):
        for k in range(4):
            @pl.when(jnp.logical_not(mine(l)))
            def _():
                for d in (1, 2, 3):
                    wz_copy(l, k, d).wait_send()
                gy_copy(l, k).wait_send()

            for d in (1, 2, 3):
                gz_copy(l, k, d).wait_send()

        for d in (1, 2, 3):
            sx_copy(l, d).wait_send()
            sz_copy(l, d).wait_send()
            sy_copy(l, d).wait_send()
        sc_copy(l).wait_send()

    @pl.when(diag)
    def _():
        for k in range(4):
            for d in (1, 2, 3):
                fz_copy(k, d).wait_send()
            for d in range(4):
                fc_copy(k, d).wait_send()

    small_out.wait()
    lo_out.wait()
    ig_out.wait()
    for k in range(4):
        pltpu.make_async_copy(final[k], outs[k], st.at[k]).wait()


WSHAPES = ((3, D, 128), (128, D), (D, FFS), (FFS, D))
PSHAPES = ((3, 256, 128), (32, D), (256, FFS), (128, D))


def run(*operands):
    vm = pltpu.VMEM
    scratch = [vm((8, D), F32), vm((2, 8, SEQ), jnp.int32)]
    scratch += [vm((2, *shape), BF) for shape in WSHAPES]
    scratch += [vm((2, 8, D), F32)]
    scratch += [vm((2, SEQ, D), BF)] * 2 + [vm((SEQ, D), BF)] * 2
    scratch += [vm((4, 4, BLK, D), BF)] * 2 + [vm((4, BLK, D), BF)] * 2 + [vm((4, 128, D), F32)]
    scratch += [
        vm((2, 3, SEQ, 128), BF),
        vm((2, SEQ, 128), BF),
        vm((2, 2, SEQ, SEQ), BF),
        vm((2, SEQ, FFS), F32),
        vm((2, SEQ, FFS), BF),
        vm((2, BLK, D), F32),
        vm((2, BLK, D), F32),
        vm((2, BLK, 128), F32),
        vm((2, BLK, 128), F32),
        vm((BLK, D), F32),
        vm((BLK, D), F32),
    ]
    scratch += [
        vm((8, SEQ), jnp.int32),
        vm((SEQ, SEQ), F32),
        vm((BLK, D), BF),
        vm((SEQ, FFS), BF),
        vm((2, SEQ, 128), F32),
        vm((3, SEQ, 128), BF),
    ]
    scratch += [vm((2, BLK, D), BF)] * 4 + [vm((2, 8, D), F32)]
    scratch += [vm((2, n, 8, D), F32) for n in (4, 2, 4, 4)] + [vm((8, D), F32)]
    scratch += [vm((2, *shape), BF) for shape in WSHAPES]
    scratch += [vm((2, 3, *shape), BF) for shape in PSHAPES]
    scratch += [vm((2, *shape), BF) for shape in PSHAPES]
    scratch += [vm((3, *shape), BF) for shape in PSHAPES]
    scratch += [vm(shape, BF) for shape in WSHAPES]
    dma = pltpu.SemaphoreType.DMA
    scratch += [dma((3,)), dma((3,)), dma((5, 4)), dma((2, 5)), dma((2, 4, 4)), dma((2, 4, 4)), dma((5,))]
    scratch += [dma((4, 4))] * 8
    scratch += [dma((2,))] * 4
    scratch += [dma((2, 4, 4)), dma((2, 4, 4)), dma((2, 4)), dma((4, 4))]
    scratch += [dma((4, 4))] * 4 + [dma((7,))]
    scratch += [dma((2, 4))] * 2 + [dma((2,))] * 2 + [dma((2, 4))] * 4
    any_space = pl.BlockSpec(memory_space=pl.ANY)
    in_vmem = pl.BlockSpec(memory_space=pltpu.VMEM)
    return pl.pallas_call(
        kernel,
        out_shape=[
            jax.ShapeDtypeStruct((2, BLK, D), BF),
            jax.ShapeDtypeStruct((2, BLK, D), BF),
            *(jax.ShapeDtypeStruct(shape, BF) for shape in WSHAPES),
            jax.ShapeDtypeStruct((8, D), F32),
        ],
        in_specs=[any_space] * 2 + [in_vmem] + [any_space] * 4 + [in_vmem] * 8,
        out_specs=[any_space] * 7,
        scratch_shapes=scratch,
        compiler_params=pltpu.CompilerParams(
            collective_id=0, has_side_effects=True, vmem_limit_bytes=60 * 1024 * 1024
        ),
    )(*operands)


def local(
    inputs, segments, qkv_weight, qv_bias, out_weight, out_bias, gain_one, shift_one,
    up_weight, up_bias, down_weight, down_bias, gain_two, shift_two, cotangent,
):
    lo, ig, gq, go, gu, gd, gs = run(
        inputs[:, 0], cotangent[:, 0], segments,
        qkv_weight[0], out_weight[0], up_weight[0], down_weight[0],
        out_bias, gain_one, shift_one, down_bias, gain_two, shift_two, up_bias, qv_bias,
    )
    return (
        lo[None, :, None],
        ig[None, :, None],
        gq[None].astype(F32),
        gs[6, 512:768].reshape(1, 2, 128),
        go[None].astype(F32),
        gs[0:1],
        gs[1:2],
        gs[2:3],
        gu[None].astype(F32),
        gs[6:7, 0:512],
        gd[None].astype(F32),
        gs[3:4],
        gs[4:5],
        gs[5:6],
    )


def solution(mesh):
    fine = Mesh(mesh.devices.reshape(2, 4, 2, 4, 2), ("s", "x", "yh", "z", "c"))
    t = ("x", "yh")
    dp = ("z", "c")
    return jax.shard_map(
        local,
        mesh=fine,
        in_specs=(
            P(None, dp, t, None),
            P(None, dp, None),
            P("s", None, None, t),
            P("s", None, t),
            P("s", t, None),
            P("s", None),
            P("s", None),
            P("s", None),
            P("s", None, t),
            P("s", t),
            P("s", t, None),
            P("s", None),
            P("s", None),
            P("s", None),
            P(None, dp, t, None),
        ),
        out_specs=(
            P("s", None, dp, t, None),
            P("s", None, dp, t, None),
            P("s", None, None, t),
            P("s", None, t),
            P("s", t, None),
            P("s", None),
            P("s", None),
            P("s", None),
            P("s", None, t),
            P("s", t),
            P("s", t, None),
            P("s", None),
            P("s", None),
            P("s", None),
        ),
        check_vma=False,
    )
```

```python
import jax
import jax.numpy as jnp
from jax import lax
from jax.experimental import pallas as pl
from jax.experimental.pallas import tpu as pltpu
from jax.sharding import Mesh
from jax.sharding import PartitionSpec as P


BF = jnp.bfloat16
F32 = jnp.float32
MESH = pl.DeviceIdType.MESH
D = 1024
FFS = 512
SEQ = 512
BLK = 64
HALF = 32
QKV, OUT, UP, DOWN = 0, 1, 2, 3
PIECE = (256, 32, 256, 128)
FA, FM, BM, BA = 0, 1, 2, 3


def remote(src, dst, send, recv, dev):
    return pltpu.make_async_remote_copy(
        src_ref=src, dst_ref=dst, send_sem=send, recv_sem=recv, device_id=dev, device_id_type=MESH
    )


def dot_nn(a, b):
    return lax.dot_general(a, b, (((1,), (0,)), ((), ())), preferred_element_type=F32)


def dot_nt(a, b):
    return lax.dot_general(a, b, (((1,), (1,)), ((), ())), preferred_element_type=F32)


def dot_tn(a, b):
    return lax.dot_general(a, b, (((0,), (0,)), ((), ())), preferred_element_type=F32)


def normed(r):
    center = r - jnp.mean(r, axis=-1, keepdims=True)
    scale = lax.rsqrt(jnp.mean(center * center, axis=-1, keepdims=True) + 1e-06)
    return center * scale, scale


def norm_back(dy, gain, n, scale):
    e = dy * gain
    mean_e = jnp.mean(e, axis=-1, keepdims=True)
    mean_en = jnp.mean(e * n, axis=-1, keepdims=True)
    return (e - mean_e - n * mean_en) * scale


def col_sum(v):
    return jnp.sum(v, axis=0, keepdims=True)


def kernel(
    inp, cot, seg_in, wq_in, wo_in, wu_in, wd_in,
    ob_in, ga_in, sa_in, db_in, gb_in, sb_in, ub_in, qb_in,
    lo, ig, gq, go, gu, gd, gs,
    sw_in, seg,
    wq, wo, wu, wd, sw,
    hbuf, arbuf, dmbuf, dprbuf,
    ain, bin_, aout, bout, part,
    qkv, att, probs, gp, gr, n1, n2, sc1, sc2, abuf, res, dyb,
    segb, bias, cotb, dur, dacc, dx,
    yb, lob, dhb, igb, gsb, sx, sc, sz, sy, gsout,
    g0, g1, g2, g3,
    zr0, zr1, zr2, zr3,
    yo0, yo1, yo2, yo3,
    yr0, yr1, yr2, yr3,
    f0, f1, f2, f3,
    swap_s, swap_r, wy_s, wy_r, wz_s, wz_r, wl,
    ag_s, ag_r, cg_s, cg_r, ra_s, ra_r, rb_s, rb_r,
    lo_s, lo_r, ig_s, ig_r,
    gz_s, gz_r, gy_s, gy_r, fz_s, fz_r, fc_s, fc_r, st, sx_s, sx_r, sc_s, sc_r, sz_s, sz_r, sy_s, sy_r,
):
    s = lax.axis_index("s")
    x = lax.axis_index("x")
    yh = lax.axis_index("yh")
    z = lax.axis_index("z")
    c = lax.axis_index("c")
    diag = c == yh
    weights_in = (wq_in, wo_in, wu_in, wd_in)
    weights = (wq, wo, wu, wd)
    grads = (g0, g1, g2, g3)
    zrecv = (zr0, zr1, zr2, zr3)
    yout = (yo0, yo1, yo2, yo3)
    yrecv = (yr0, yr1, yr2, yr3)
    final = (f0, f1, f2, f3)
    outs = (gq, go, gu, gd)

    def at_piece(ref, k, zi, lead=()):
        rows = pl.ds(pl.multiple_of(zi * PIECE[k], PIECE[k]), PIECE[k])
        if k == QKV:
            return ref.at[(*lead, slice(None), rows)]
        return ref.at[(*lead, rows)]

    def y_dev(i):
        return {"s": lax.rem(s + i % 2, 2), "yh": lax.rem(yh + i // 2, 2)}

    def z_dev(d):
        return {"z": lax.rem(z + d, 4)}

    core = {"c": 1 - c}

    for i, ref in enumerate((ob_in, ga_in, sa_in, db_in, gb_in, sb_in)):
        sw_in[i : i + 1, :] = ref[...].astype(F32)
    sw_in[6:7, 0:512] = ub_in[...].astype(F32)
    sw_in[6:7, 512:640] = qb_in[0, 0:1, :].astype(F32)
    sw_in[6:7, 640:768] = qb_in[0, 1:2, :].astype(F32)
    for m in range(2):
        seg[m] = jnp.broadcast_to(seg_in[m], (8, SEQ))

    barrier = pltpu.get_barrier_semaphore()

    def greet(dev):
        pl.semaphore_signal(barrier, inc=1, device_id=dev, device_id_type=MESH)

    for d in (1, 2, 3):
        greet({"x": lax.rem(x + d, 4)})
        greet(z_dev(d))
        greet(y_dev(d))
    greet(core)

    @pl.when(diag)
    def _():
        pl.semaphore_wait(barrier, 10)

    @pl.when(jnp.logical_not(diag))
    def _():
        greet({"s": s, "yh": c, "c": yh})
        greet({"s": 1 - s, "yh": c, "c": yh})
        pl.semaphore_wait(barrier, 12)

    def rows_of(xi, h, ci):
        return pl.ds(pl.multiple_of(xi * 128 + h * BLK + ci * HALF, HALF), HALF)

    mirror = {"yh": c, "c": yh}
    swaps = (
        (inp.at[s, pl.ds(0, HALF)], hbuf.at[0, rows_of(x, 0, yh)]),
        (inp.at[s, pl.ds(HALF, HALF)], hbuf.at[0, rows_of(x, 1, yh)]),
        (seg.at[s], segb),
        (cot.at[s], cotb),
    )

    def swap_start(i):
        src, dst = swaps[i]

        @pl.when(diag)
        def _():
            pltpu.make_async_copy(src, dst, swap_r.at[i]).start()

        @pl.when(jnp.logical_not(diag))
        def _():
            remote(src, dst, swap_s.at[i], swap_r.at[i], mirror).start()

    def swap_wait(i):
        src, dst = swaps[i]

        @pl.when(diag)
        def _():
            pltpu.make_async_copy(src, dst, swap_r.at[i]).wait()

        @pl.when(jnp.logical_not(diag))
        def _():
            remote(src, dst, swap_s.at[i], swap_r.at[i], mirror).wait()

    def wy_copy(k, i):
        if k == 4:
            return remote(sw_in, sw.at[s], wy_s.at[k, i], wy_r.at[s, k], y_dev(i))
        src = at_piece(weights_in[k], k, z)
        return remote(src, at_piece(weights[k], k, z, (s,)), wy_s.at[k, i], wy_r.at[s, k], y_dev(i))

    def wy_arrival(l, k):
        if k == 4:
            return remote(sw_in, sw.at[l], wy_s.at[k, 0], wy_r.at[l, k], core)
        dst = at_piece(weights[k], k, z, (l,))
        return remote(dst, dst, wy_s.at[k, 0], wy_r.at[l, k], core)

    def wl_copy(k):
        if k == 4:
            return pltpu.make_async_copy(sw_in, sw.at[s], wl.at[k])
        return pltpu.make_async_copy(weights_in[k], weights[k].at[s], wl.at[k])

    def wz_copy(l, k, d):
        piece = at_piece(weights[k], k, z, (l,))
        return remote(piece, piece, wz_s.at[l, k, d], wz_r.at[l, k, d], z_dev(d))

    def wz_arrival(l, k, d):
        piece = at_piece(weights[k], k, lax.rem(z + 4 - d, 4), (l,))
        return remote(piece, piece, wz_s.at[l, k, d], wz_r.at[l, k, d], z_dev(d))

    def mine(l):
        return jnp.logical_and(diag, s == l)

    def relay(l, k):
        @pl.when(jnp.logical_not(mine(l)))
        def _():
            wy_arrival(l, k).wait_recv()
            if k != 4:
                for d in (1, 3, 2):
                    wz_copy(l, k, d).start()

    def ready(l, k):
        @pl.when(mine(l))
        def _():
            wl_copy(k).wait()

        @pl.when(jnp.logical_not(mine(l)))
        def _():
            for d in (1, 3, 2):
                wz_arrival(l, k, d).wait_recv()

    def spread(k):
        @pl.when(diag)
        def _():
            for i in (1, 3, 2):
                wy_copy(k, i).start()
            wl_copy(k).start()

    swap_start(0)
    swap_start(1)
    spread(4)
    spread(QKV)
    swap_start(2)
    spread(OUT)
    spread(UP)
    spread(DOWN)
    swap_start(3)

    def arrival(i):
        return i + (i // 2) * (5 - 2 * i)

    def reversed_arrival(i):
        return arrival(3 - i)

    def ag_direct(ph, view, h, d):
        block = view.at[rows_of(x, h, c)]
        sem = 4 * h + d
        return remote(block, block, ag_s.at[ph, sem], ag_r.at[ph, sem], {"x": lax.rem(x + d, 4)})

    def ag_forward(ph, view, h, d):
        block = view.at[rows_of(lax.rem(x + 4 - d, 4), h, c)]
        return remote(block, block, cg_s.at[ph, 4 * h + d], cg_r.at[ph, 4 * h + d], core)

    def ag_start(ph, view, h):
        for d in (1, 3, 2):
            ag_direct(ph, view, h, d).start()
        ag_forward(ph, view, h, 0).start()

    def block_rows(h, d):
        return pl.ds(pl.multiple_of(lax.rem(x + 4 - d, 4) * 128 + h * BLK, BLK), BLK)

    def pair_rows(t, order):
        h = t // 2
        i = 2 * (t - 2 * h)
        return block_rows(h, order(i)), block_rows(h, order(i + 1))

    def load(ref, lead, pair):
        return jnp.concatenate([ref[(*lead, at, slice(None))] for at in pair], axis=0)

    def store(ref, lead, pair, value):
        for i, at in enumerate(pair):
            ref[(*lead, at, slice(None))] = value[i * BLK : (i + 1) * BLK]

    def ag_pair(ph, view, t):
        h = t // 2

        @pl.when(t == 2 * h)
        def _():
            for d in (1, 3):
                ag_direct(ph, view, h, d).wait_recv()
                ag_forward(ph, view, h, d).start()

        @pl.when(t != 2 * h)
        def _():
            ag_direct(ph, view, h, 2).wait_recv()
            ag_forward(ph, view, h, 2).start()

        i = 2 * (t - 2 * h)
        ag_forward(ph, view, h, arrival(i)).wait_recv()
        ag_forward(ph, view, h, arrival(i + 1)).wait_recv()
        return pair_rows(t, arrival)

    def ag_end(ph, view):
        for h in range(2):
            for d in (1, 2, 3):
                ag_direct(ph, view, h, d).wait_send()
            for d in range(4):
                ag_forward(ph, view, h, d).wait_send()

    my_half = pl.ds(pl.multiple_of(c * HALF, HALF), HALF)
    other_half = pl.ds(pl.multiple_of((1 - c) * HALF, HALF), HALF)

    def ra_copy(ph, slot):
        return remote(aout.at[slot], ain.at[ph, slot], ra_s.at[ph, slot], ra_r.at[ph, slot], core)

    def rb_copy(ph, slot):
        target = {"x": lax.rem(x + 8 - slot, 4)}
        return remote(bout.at[slot], bin_.at[ph, slot], rb_s.at[ph, slot], rb_r.at[ph, slot], target)

    def rs_begin(ph, slot, value):
        part[slot] = value
        aout[slot] = part[slot, other_half, :].astype(BF)
        ra_copy(ph, slot).start()

    def rs_pass(ph, h, d):
        slot = 4 * h + d
        ra_copy(ph, slot).wait_recv()
        total = part[slot, my_half, :] + ain[ph, slot].astype(F32)

        @pl.when(d == 0)
        def _():
            res[h] = total

        @pl.when(d != 0)
        def _():
            bout[slot] = total.astype(BF)
            rb_copy(ph, slot).start()

    def rs_loop(ph, order, step):
        def one(t, carry):
            @pl.when(t < 4)
            def _():
                h = t // 2
                value = step(t)
                for i in range(2):
                    d = order(2 * (t - 2 * h) + i)
                    rs_begin(ph, 4 * h + d, value[i * BLK : (i + 1) * BLK])

            @pl.when(t > 0)
            def _():
                h = (t - 1) // 2
                for i in range(2):
                    rs_pass(ph, h, order(2 * (t - 1 - 2 * h) + i))

            return carry

        lax.fori_loop(0, 5, one, 0)

    def rs_end(ph, h):
        total = res[h]
        for d in (1, 3, 2):
            slot = 4 * h + d
            rb_copy(ph, slot).wait_recv()
            total = total + bin_[ph, slot].astype(F32)
        for d in range(4):
            ra_copy(ph, 4 * h + d).wait_send()
        for d in (1, 2, 3):
            rb_copy(ph, 4 * h + d).wait_send()
        return total

    lanes = lax.broadcasted_iota(jnp.int32, (1, 128), 1) < 64
    head_mask = (
        lanes.astype(F32).astype(BF),
        (1.0 - lanes.astype(F32)).astype(BF),
    )
    first_head = lax.broadcasted_iota(jnp.int32, (128, 128), 1) < 64

    def home_copy(l, src, dst, send, recv):
        return remote(src.at[l], dst.at[s], send.at[l], recv.at[s], {"s": l, "yh": c, "c": yh})

    def home_start(l, src, dst, send, recv):
        @pl.when(mine(l))
        def _():
            dst[s] = src[l]

        @pl.when(jnp.logical_not(mine(l)))
        def _():
            home_copy(l, src, dst, send, recv).start()

    def home_wait(src, dst, send, recv):
        for l in range(2):
            @pl.when(jnp.logical_not(mine(l)))
            def _():
                home_copy(l, src, dst, send, recv).wait_send()
                remote(src.at[l], dst.at[l], send.at[l], recv.at[l], core).wait_recv()

    for h in range(2):
        swap_wait(h)
        ag_start(FA, hbuf.at[0], h)
    relay(0, 4)
    relay(0, QKV)
    relay(1, 4)

    @pl.when(diag)
    def _():
        wl_copy(4).wait()

    swap_wait(2)
    documents = lax.broadcasted_iota(jnp.int32, (8, SEQ), 0) == segb[...]
    documents = documents.astype(F32).astype(BF)
    put = lax.broadcasted_iota(jnp.int32, (SEQ, SEQ), 1)
    put = put - lax.rem(put, 128) + lax.rem(put, 64) // 32 * 64 + lax.rem(put, 128) // 64 * 32 + lax.rem(put, 32)
    move = lax.broadcasted_iota(jnp.int32, (SEQ, SEQ), 0) == put
    documents = dot_nn(documents, move.astype(F32).astype(BF)).astype(BF)
    bias[...] = jnp.where(dot_tn(documents, documents) > 0.5, 0.0, -1e30)

    def forward(l, carry):
        small = sw[l]
        out_b, gain_a, shift_a = small[0:1], small[1:2], small[2:3]
        down_b, gain_b, shift_b = small[3:4], small[4:5], small[5:6]
        view = hbuf.at[l]
        ready(l, QKV)

        def project(t, carry):
            at = ag_pair(FA, view, t)
            rows = load(hbuf, (l,), at)
            q = dot_nn(rows, wq[l, 0]) + sw[l, 6:7, 512:640]
            k = dot_nn(rows, wq[l, 1])
            v = dot_nn(rows, wq[l, 2]) + sw[l, 6:7, 640:768]
            store(qkv, (l, 0), at, q.astype(BF))
            store(qkv, (l, 1), at, k.astype(BF))
            store(qkv, (l, 2), at, v.astype(BF))
            return carry

        lax.fori_loop(0, 4, project, 0)

        @pl.when(l == 0)
        def _():
            relay(0, OUT)
            relay(0, UP)

        ready(l, OUT)

        def attend(t):
            at = pair_rows(t, reversed_arrival)
            q = load(qkv, (l, 0), at)
            mask = load(bias, (), at)
            keys = qkv[l, 1]
            values = qkv[l, 2]
            heads = []
            for j in range(2):
                scores = dot_nt(q * head_mask[j], keys) * 0.125 + mask
                e = jnp.exp(scores - jnp.max(scores, axis=-1, keepdims=True))
                p = (e * (1.0 / jnp.sum(e, axis=-1, keepdims=True))).astype(BF)
                store(probs, (l, j), at, p)
                heads.append(dot_nn(p, values))
            block = jnp.where(first_head, heads[0], heads[1]).astype(BF)
            store(att, (l,), at, block)
            return dot_nn(block, wo[l])

        rs_loop(FA, reversed_arrival, attend)

        @pl.when(l == 0)
        def _():
            relay(0, DOWN)
            for k in (QKV, OUT, UP, DOWN):
                relay(1, k)

        ar_view = arbuf.at[l]
        for h in range(2):
            r1 = hbuf[l, rows_of(x, h, c), :].astype(F32) + rs_end(FA, h) + out_b
            n, scale = normed(r1)
            n1[l, h] = n
            sc1[l, h] = jnp.broadcast_to(scale, (HALF, 128))
            a = n * gain_a + shift_a
            abuf[h] = a
            arbuf[l, rows_of(x, h, c), :] = a.astype(BF)
            ag_start(FM, ar_view, h)
        ag_end(FA, view)
        ready(l, UP)
        ready(l, DOWN)

        def feed(t):
            at = ag_pair(FM, ar_view, t)
            u = dot_nn(load(arbuf, (l,), at), wu[l]) + sw[l, 6:7, 0:512]
            cdf = 0.5 * (1.0 + lax.erf(u * 0.7071067811865476))
            store(gp, (l,), at, cdf + u * (jnp.exp(-0.5 * u * u) * 0.3989422804014327))
            g = (u * cdf).astype(BF)
            store(gr, (l,), at, g)
            return dot_nn(g, wd[l])

        rs_loop(FM, arrival, feed)
        for h in range(2):
            r2 = abuf[h] + rs_end(FM, h) + down_b
            n, scale = normed(r2)
            n2[l, h] = n
            sc2[l, h] = jnp.broadcast_to(scale, (HALF, 128))
            y = (n * gain_b + shift_b).astype(BF)
            yb[l, h * HALF : (h + 1) * HALF, :] = y

            @pl.when(l == 0)
            def _():
                hbuf[1, rows_of(x, h, c), :] = y
                ag_start(FA, hbuf.at[1], h)

        ag_end(FM, ar_view)
        home_start(l, yb, lob, lo_s, lo_r)
        return carry

    lax.fori_loop(0, 2, forward, 0)

    def gz_copy(l, k, d):
        src = at_piece(grads[k], k, lax.rem(z + d, 4), (l,))
        return remote(src, zrecv[k].at[l, d - 1], gz_s.at[l, k, d], gz_r.at[l, k, d], z_dev(d))

    def gz_start(l, k):
        for d in (1, 3, 2):
            gz_copy(l, k, d).start()

    def gy_copy(l, k):
        slot = 2 * lax.rem(yh + 2 - c, 2) + lax.rem(s + 2 - l, 2)
        return remote(
            yout[k].at[l], yrecv[k].at[slot - 1], gy_s.at[l, k], gy_r.at[k, slot], {"s": l, "yh": c}
        )

    def gy_start(l, k):
        total = at_piece(grads[k], k, z, (l,))[...].astype(F32)
        for d in (1, 3, 2):
            gz_copy(l, k, d).wait_recv()
            total = total + zrecv[k][l, d - 1].astype(F32)
        yout[k][l] = total.astype(BF)

        @pl.when(jnp.logical_not(mine(l)))
        def _():
            gy_copy(l, k).start()

    def fz_copy(k, d):
        piece = at_piece(final[k], k, z)
        return remote(piece, piece, fz_s.at[k, d], fz_r.at[k, d], z_dev(d))

    def fc_copy(k, d):
        piece = at_piece(final[k], k, lax.rem(z + 4 - d, 4))
        return remote(piece, piece, fc_s.at[k, d], fc_r.at[k, d], core)

    def fz_start(k):
        @pl.when(diag)
        def _():
            total = yout[k][s].astype(F32)
            for i in (1, 2, 3):
                remote(
                    yrecv[k].at[i - 1], yrecv[k].at[i - 1], gy_s.at[0, k], gy_r.at[k, i], core
                ).wait_recv()
                total = total + yrecv[k][i - 1].astype(F32)
            at_piece(final[k], k, z)[...] = total.astype(BF)
            for d in (1, 3, 2):
                fz_copy(k, d).start()
            fc_copy(k, 0).start()

    def fc_start(k):
        @pl.when(diag)
        def _():
            for d in (1, 3, 2):
                piece = at_piece(final[k], k, lax.rem(z + 4 - d, 4))
                remote(piece, piece, fz_s.at[k, d], fz_r.at[k, d], z_dev(d)).wait_recv()
                fc_copy(k, d).start()

    def out_start(k):
        @pl.when(jnp.logical_not(diag))
        def _():
            for d in range(4):
                fc_copy(k, d).wait_recv()

        pltpu.make_async_copy(final[k], outs[k], st.at[k]).start()

    def sx_copy(l, d):
        return remote(gsb.at[l], sx.at[l, x], sx_s.at[l, d], sx_r.at[l, d], {"x": lax.rem(x + d, 4)})

    def sc_copy(l):
        return remote(sc.at[l, c], sc.at[l, c], sc_s.at[l], sc_r.at[l], core)

    def sz_copy(l, d):
        return remote(sz.at[l, z], sz.at[l, z], sz_s.at[l, d], sz_r.at[l, d], z_dev(d))

    def sy_copy(l, i):
        block = sy.at[l, 2 * yh + s]
        return remote(block, block, sy_s.at[l, i], sy_r.at[l, i], y_dev(i))

    def small_x(l):
        sx[l, x] = gsb[l]
        for d in (1, 3, 2):
            sx_copy(l, d).start()

    def small_core(l):
        for d in (1, 3, 2):
            sx_copy(l, d).wait_recv()
        sc[l, c] = ((sx[l, 0] + sx[l, 1]) + sx[l, 2]) + sx[l, 3]
        sc[l, c, 6:7, :] = gsb[l, 6:7, :]
        sc_copy(l).start()

    def small_z(l):
        sc_copy(l).wait_recv()
        sz[l, z] = sc[l, 0] + sc[l, 1]
        sz[l, z, 6:7, :] = sc[l, 0, 6:7, :]
        sz[l, z, 7:8, :] = sc[l, 1, 6:7, :]
        for d in (1, 3, 2):
            sz_copy(l, d).start()

    def small_y(l):
        for d in (1, 3, 2):
            sz_copy(l, d).wait_recv()
        sy[l, 2 * yh + s] = ((sz[l, 0] + sz[l, 1]) + sz[l, 2]) + sz[l, 3]
        for i in (1, 3, 2):
            sy_copy(l, i).start()

    def small_end():
        for l in range(2):
            for i in (1, 3, 2):
                sy_copy(l, i).wait_recv()
        gsout[...] = ((sy[s, 0] + sy[s, 1]) + sy[s, 2]) + sy[s, 3]

        @pl.when(yh == 1)
        def _():
            gsout[6:7, :] = gsout[7:8, :]

    swap_wait(3)

    def input_grad(l, h):
        low = (abuf[h] + rs_end(BA, h)).astype(BF)
        dhb[l, h * HALF : (h + 1) * HALF, :] = low
        return low.astype(F32)

    def grads_qkv(l):
        def some(i, carry):
            cols = pl.ds(pl.multiple_of(i * 128, 128), 128)
            rows = hbuf[l, :, cols]
            for j in range(3):
                g0[l, j, cols, :] = dot_tn(rows, dx[j]).astype(BF)
            return carry

        lax.fori_loop(0, 8, some, 0)
        gz_start(l, QKV)

    def grads_out(l):
        g1[l] = dot_tn(att[l], dprbuf[...]).astype(BF)
        gz_start(l, OUT)

    def grads_down(l):
        def some(i, carry):
            cols = pl.ds(pl.multiple_of(i * 128, 128), 128)
            g3[l, cols, :] = dot_tn(gr[l, :, cols], dmbuf[...]).astype(BF)
            return carry

        lax.fori_loop(0, 4, some, 0)
        gz_start(l, DOWN)

    def grads_up(l):
        def some(i, carry):
            cols = pl.ds(pl.multiple_of(i * 128, 128), 128)
            g2[l, cols, :] = dot_tn(arbuf[l, :, cols], dur[...]).astype(BF)
            return carry

        lax.fori_loop(0, 8, some, 0)
        gz_start(l, UP)

    def backward(step_index, carry):
        l = 1 - step_index
        small = sw[l]
        gain_a, gain_b = small[1:2], small[4:5]
        gsb[l] = jnp.zeros((8, D), F32)
        for h in range(2):
            @pl.when(l == 1)
            def _():
                dyb[...] = cotb[h * HALF : (h + 1) * HALF, :].astype(F32)

            @pl.when(l == 0)
            def _():
                dyb[...] = input_grad(1, h)

            dy = dyb[...]
            n = n2[l, h]
            dr2 = norm_back(dy, gain_b, n, sc2[l, h, :, 0:1])
            dmbuf[rows_of(x, h, c), :] = dr2.astype(BF)
            ag_start(BM, dmbuf, h)
            abuf[h] = dr2
            gsb[l, 4:5, :] += col_sum(dy * n)
            gsb[l, 5:6, :] += col_sum(dy)
            gsb[l, 3:4, :] += col_sum(dr2)

            @pl.when(l == 0)
            def _():
                if h == 0:
                    grads_qkv(1)
                else:
                    grads_out(1)
                    small_z(1)
                    ag_end(BA, dprbuf)
                    home_start(1, dhb, igb, ig_s, ig_r)

        def feed_back(t):
            at = ag_pair(BM, dmbuf, t)
            dg = dot_nt(load(dmbuf, (), at), wd[l])
            du = dg * load(gp, (l,), at)
            gsb[l, 6:7, 0:512] += col_sum(du)
            low = du.astype(BF)
            store(dur, (), at, low)
            return dot_nt(low, wu[l])

        rs_loop(BM, arrival, feed_back)
        for h in range(2):
            da = abuf[h] + rs_end(BM, h)
            n = n1[l, h]
            dr1 = norm_back(da, gain_a, n, sc1[l, h, :, 0:1])
            dprbuf[rows_of(x, h, c), :] = dr1.astype(BF)
            ag_start(BA, dprbuf, h)
            abuf[h] = dr1
            gsb[l, 1:2, :] += col_sum(da * n)
            gsb[l, 2:3, :] += col_sum(da)
            gsb[l, 0:1, :] += col_sum(dr1)
            if h == 0:
                grads_down(l)
            else:
                grads_up(l)
        ag_end(BM, dmbuf)
        dacc[...] = jnp.zeros_like(dacc)

        @pl.when(l == 0)
        def _():
            small_y(1)
            for k in (DOWN, UP):
                gy_start(1, k)

        def attend_back(t, carry):
            at = ag_pair(BA, dprbuf, t)
            grad = dot_nt(load(dprbuf, (), at), wo[l]).astype(BF)
            q = load(qkv, (l, 0), at)
            keys = qkv[l, 1]
            values = qkv[l, 2]
            heads = []
            dk = dacc[0]
            dv = dacc[1]
            for j in range(2):
                own = grad * head_mask[j]
                low_p = load(probs, (l, j), at)
                p = low_p.astype(F32)
                dp = dot_nt(own, values)
                ds = (p * (dp - jnp.sum(p * dp, axis=-1, keepdims=True))).astype(BF)
                heads.append(dot_nn(ds, keys))
                dk = dk + dot_tn(ds, q * head_mask[j])
                dv = dv + dot_tn(low_p, own)
            dacc[0] = dk
            dacc[1] = dv
            dq = (jnp.where(first_head, heads[0], heads[1]) * 0.125).astype(BF)
            store(dx, (0,), at, dq)
            gsb[l, 6:7, 512:640] += col_sum(dq.astype(F32))
            return carry

        lax.fori_loop(0, 4, attend_back, 0)
        dx[1] = (dacc[0] * 0.125).astype(BF)
        dv = dacc[1].astype(BF)
        dx[2] = dv
        gsb[l, 6:7, 640:768] = col_sum(dv.astype(F32))
        small_x(l)

        def input_back(t):
            at = pair_rows(t, reversed_arrival)
            return (
                dot_nt(load(dx, (0,), at), wq[l, 0])
                + dot_nt(load(dx, (1,), at), wq[l, 1])
                + dot_nt(load(dx, (2,), at), wq[l, 2])
            )

        rs_loop(BA, reversed_arrival, input_back)
        small_core(l)
        return carry

    lax.fori_loop(0, 2, backward, 0)
    grads_qkv(0)
    grads_out(0)
    small_z(0)
    for h in range(2):
        input_grad(0, h)
    ag_end(BA, dprbuf)
    home_start(0, dhb, igb, ig_s, ig_r)
    small_y(0)

    for k in (QKV, OUT):
        gy_start(1, k)
    for k in (DOWN, UP):
        gy_start(0, k)
    for k in (DOWN, UP):
        fz_start(k)
    for k in (QKV, OUT):
        gy_start(0, k)
    for k in (DOWN, UP):
        fc_start(k)
    for k in (QKV, OUT):
        fz_start(k)
    home_wait(yb, lob, lo_s, lo_r)
    lo_out = pltpu.make_async_copy(lob, lo, st.at[5])
    lo_out.start()
    home_wait(dhb, igb, ig_s, ig_r)
    ig_out = pltpu.make_async_copy(igb, ig, st.at[6])
    ig_out.start()
    small_end()
    small_out = pltpu.make_async_copy(gsout, gs, st.at[4])
    small_out.start()
    for k in (DOWN, UP):
        out_start(k)
    for k in (QKV, OUT):
        fc_start(k)
    for k in (QKV, OUT):
        out_start(k)

    @pl.when(diag)
    def _():
        for k in range(5):
            for i in (1, 2, 3):
                wy_copy(k, i).wait_send()

    for l in range(2):
        for k in range(4):
            @pl.when(jnp.logical_not(mine(l)))
            def _():
                for d in (1, 2, 3):
                    wz_copy(l, k, d).wait_send()
                gy_copy(l, k).wait_send()

            for d in (1, 2, 3):
                gz_copy(l, k, d).wait_send()

        for d in (1, 2, 3):
            sx_copy(l, d).wait_send()
            sz_copy(l, d).wait_send()
            sy_copy(l, d).wait_send()
        sc_copy(l).wait_send()

    @pl.when(diag)
    def _():
        for k in range(4):
            for d in (1, 2, 3):
                fz_copy(k, d).wait_send()
            for d in range(4):
                fc_copy(k, d).wait_send()

    small_out.wait()
    lo_out.wait()
    ig_out.wait()
    for k in range(4):
        pltpu.make_async_copy(final[k], outs[k], st.at[k]).wait()


WSHAPES = ((3, D, 128), (128, D), (D, FFS), (FFS, D))
PSHAPES = ((3, 256, 128), (32, D), (256, FFS), (128, D))


def run(*operands):
    vm = pltpu.VMEM
    scratch = [vm((8, D), F32), vm((2, 8, SEQ), jnp.int32)]
    scratch += [vm((2, *shape), BF) for shape in WSHAPES]
    scratch += [vm((2, 8, D), F32)]
    scratch += [vm((2, SEQ, D), BF)] * 2 + [vm((SEQ, D), BF)] * 2
    scratch += [vm((4, 8, HALF, D), BF)] * 2 + [vm((8, HALF, D), BF)] * 2 + [vm((8, BLK, D), F32)]
    scratch += [
        vm((2, 3, SEQ, 128), BF),
        vm((2, SEQ, 128), BF),
        vm((2, 2, SEQ, SEQ), BF),
        vm((2, SEQ, FFS), F32),
        vm((2, SEQ, FFS), BF),
        vm((2, 2, HALF, D), F32),
        vm((2, 2, HALF, D), F32),
        vm((2, 2, HALF, 128), F32),
        vm((2, 2, HALF, 128), F32),
        vm((2, HALF, D), F32),
        vm((2, HALF, D), F32),
        vm((HALF, D), F32),
    ]
    scratch += [
        vm((8, SEQ), jnp.int32),
        vm((SEQ, SEQ), F32),
        vm((BLK, D), BF),
        vm((SEQ, FFS), BF),
        vm((2, SEQ, 128), F32),
        vm((3, SEQ, 128), BF),
    ]
    scratch += [vm((2, BLK, D), BF)] * 4 + [vm((2, 8, D), F32)]
    scratch += [vm((2, n, 8, D), F32) for n in (4, 2, 4, 4)] + [vm((8, D), F32)]
    scratch += [vm((2, *shape), BF) for shape in WSHAPES]
    scratch += [vm((2, 3, *shape), BF) for shape in PSHAPES]
    scratch += [vm((2, *shape), BF) for shape in PSHAPES]
    scratch += [vm((3, *shape), BF) for shape in PSHAPES]
    scratch += [vm(shape, BF) for shape in WSHAPES]
    dma = pltpu.SemaphoreType.DMA
    scratch += [dma((4,)), dma((4,)), dma((5, 4)), dma((2, 5)), dma((2, 4, 4)), dma((2, 4, 4)), dma((5,))]
    scratch += [dma((4, 8))] * 8
    scratch += [dma((2,))] * 4
    scratch += [dma((2, 4, 4)), dma((2, 4, 4)), dma((2, 4)), dma((4, 4))]
    scratch += [dma((4, 4))] * 4 + [dma((7,))]
    scratch += [dma((2, 4))] * 2 + [dma((2,))] * 2 + [dma((2, 4))] * 4
    any_space = pl.BlockSpec(memory_space=pl.ANY)
    in_vmem = pl.BlockSpec(memory_space=pltpu.VMEM)
    return pl.pallas_call(
        kernel,
        out_shape=[
            jax.ShapeDtypeStruct((2, BLK, D), BF),
            jax.ShapeDtypeStruct((2, BLK, D), BF),
            *(jax.ShapeDtypeStruct(shape, BF) for shape in WSHAPES),
            jax.ShapeDtypeStruct((8, D), F32),
        ],
        in_specs=[any_space] * 2 + [in_vmem] + [any_space] * 4 + [in_vmem] * 8,
        out_specs=[any_space] * 7,
        scratch_shapes=scratch,
        compiler_params=pltpu.CompilerParams(
            collective_id=0, has_side_effects=True, vmem_limit_bytes=60 * 1024 * 1024
        ),
    )(*operands)


def finish_kernel(lo, ig, gq, go, gu, gd, gs, lo_o, ig_o, gq_o, qv_o, go_o, ob_o, ga_o, sa_o, gu_o, ub_o, gd_o, db_o, gb_o, sb_o):
    lo_o[0, :, 0] = lo[...]
    ig_o[0, :, 0] = ig[...]
    gq_o[0] = gq[...].astype(F32)
    go_o[0] = go[...].astype(F32)
    gu_o[0] = gu[...].astype(F32)
    gd_o[0] = gd[...].astype(F32)
    for row, ref in enumerate((ob_o, ga_o, sa_o, db_o, gb_o, sb_o)):
        ref[...] = gs[row : row + 1, :]
    ub_o[...] = gs[6:7, 0:512]
    qv_o[0, 0:1, :] = gs[6:7, 512:640]
    qv_o[0, 1:2, :] = gs[6:7, 640:768]


def finish(lo, ig, *rest):
    steps = 4
    row = ((1, D), lambda i: (0, 0))
    wide = ((2, BLK // steps, D), lambda i: (0, i, 0))
    wide_out = ((1, 2, 1, BLK // steps, D), lambda i: (0, 0, 0, i, 0))
    wmaps = ((lambda i: (0, i, 0)), (lambda i: (i, 0)), (lambda i: (i, 0)), (lambda i: (i, 0)))
    omaps = ((lambda i: (0, 0, i, 0)),) + ((lambda i: (0, i, 0)),) * 3
    gq_o, go_o, gu_o, gd_o = (((1, *shape), m) for shape, m in zip(PSHAPES, omaps))
    specs_in = [wide, wide, *zip(PSHAPES, wmaps), ((8, D), lambda i: (0, 0))]
    specs_out = [
        wide_out, wide_out, gq_o, ((1, 2, 128), lambda i: (0, 0, 0)), go_o, row, row, row,
        gu_o, ((1, FFS), lambda i: (0, 0)), gd_o, row, row, row,
    ]
    full = [
        ((1, 2, 1, BLK, D), BF), ((1, 2, 1, BLK, D), BF), ((1, 3, D, 128), F32), ((1, 2, 128), F32),
        ((1, 128, D), F32), ((1, D), F32), ((1, D), F32), ((1, D), F32), ((1, D, FFS), F32),
        ((1, FFS), F32), ((1, FFS, D), F32), ((1, D), F32), ((1, D), F32), ((1, D), F32),
    ]
    return pl.pallas_call(
        finish_kernel,
        grid=(steps,),
        out_shape=[jax.ShapeDtypeStruct(*leaf) for leaf in full],
        in_specs=[pl.BlockSpec(*spec) for spec in specs_in],
        out_specs=[pl.BlockSpec(*spec) for spec in specs_out],
        compiler_params=pltpu.CompilerParams(vmem_limit_bytes=60 * 1024 * 1024),
    )(lo, ig, *rest)


def local(
    inputs, segments, qkv_weight, qv_bias, out_weight, out_bias, gain_one, shift_one,
    up_weight, up_bias, down_weight, down_bias, gain_two, shift_two, cotangent,
):
    results = run(
        inputs[:, 0], cotangent[:, 0], segments,
        qkv_weight[0], out_weight[0], up_weight[0], down_weight[0],
        out_bias, gain_one, shift_one, down_bias, gain_two, shift_two, up_bias, qv_bias,
    )
    return tuple(finish(*results))


def solution(mesh):
    fine = Mesh(mesh.devices.reshape(2, 4, 2, 4, 2), ("s", "x", "yh", "z", "c"))
    t = ("x", "yh")
    dp = ("z", "c")
    return jax.shard_map(
        local,
        mesh=fine,
        in_specs=(
            P(None, dp, t, None),
            P(None, dp, None),
            P("s", None, None, t),
            P("s", None, t),
            P("s", t, None),
            P("s", None),
            P("s", None),
            P("s", None),
            P("s", None, t),
            P("s", t),
            P("s", t, None),
            P("s", None),
            P("s", None),
            P("s", None),
            P(None, dp, t, None),
        ),
        out_specs=(
            P("s", None, dp, t, None),
            P("s", None, dp, t, None),
            P("s", None, None, t),
            P("s", None, t),
            P("s", t, None),
            P("s", None),
            P("s", None),
            P("s", None),
            P("s", None, t),
            P("s", t),
            P("s", t, None),
            P("s", None),
            P("s", None),
            P("s", None),
        ),
        check_vma=False,
    )
```

```python
import jax
import jax.numpy as jnp
from jax import lax
from jax.experimental import pallas as pl
from jax.experimental.pallas import tpu as pltpu
from jax.sharding import Mesh
from jax.sharding import PartitionSpec as P


BF = jnp.bfloat16
F32 = jnp.float32
MESH = pl.DeviceIdType.MESH
D = 1024
FFS = 512
SEQ = 512
BLK = 64
HALF = 32
QKV, OUT, UP, DOWN = 0, 1, 2, 3
PIECE = (256, 32, 256, 128)
FA, FM, BM, BA = 0, 1, 2, 3


def remote(src, dst, send, recv, dev):
    return pltpu.make_async_remote_copy(
        src_ref=src, dst_ref=dst, send_sem=send, recv_sem=recv, device_id=dev, device_id_type=MESH
    )


def dot_nn(a, b):
    return lax.dot_general(a, b, (((1,), (0,)), ((), ())), preferred_element_type=F32)


def dot_nt(a, b):
    return lax.dot_general(a, b, (((1,), (1,)), ((), ())), preferred_element_type=F32)


def dot_tn(a, b):
    return lax.dot_general(a, b, (((0,), (0,)), ((), ())), preferred_element_type=F32)


def normed(r):
    center = r - jnp.mean(r, axis=-1, keepdims=True)
    scale = lax.rsqrt(jnp.mean(center * center, axis=-1, keepdims=True) + 1e-06)
    return center * scale, scale


def norm_back(dy, gain, n, scale):
    e = dy * gain
    mean_e = jnp.mean(e, axis=-1, keepdims=True)
    mean_en = jnp.mean(e * n, axis=-1, keepdims=True)
    return (e - mean_e - n * mean_en) * scale


def col_sum(v):
    return jnp.sum(v, axis=0, keepdims=True)


def kernel(
    inp, cot, seg_in, wq_in, wo_in, wu_in, wd_in,
    ob_in, ga_in, sa_in, db_in, gb_in, sb_in, ub_in, qb_in,
    lo, ig, gq, go, gu, gd, gs,
    sw_in, seg,
    wq, wo, wu, wd, sw,
    hbuf, arbuf, dmbuf, dprbuf,
    ain, bin_, aout, bout, part,
    qkv, att, probs, gp, gr, n1, n2, sc1, sc2, abuf, res, dyb,
    segb, bias, cotb, dur, dacc, dx,
    yb, lob, dhb, igb, gsb, sx, sc, sz, sy, gsout,
    g0, g1, g2, g3,
    zr0, zr1, zr2, zr3,
    yo0, yo1, yo2, yo3,
    yr0, yr1, yr2, yr3,
    f0, f1, f2, f3,
    swap_s, swap_r, wy_s, wy_r, wz_s, wz_r, wl,
    ag_s, ag_r, cg_s, cg_r, ra_s, ra_r, rb_s, rb_r,
    lo_s, lo_r, ig_s, ig_r,
    gz_s, gz_r, gy_s, gy_r, fz_s, fz_r, fc_s, fc_r, st, sx_s, sx_r, sc_s, sc_r, sz_s, sz_r, sy_s, sy_r,
):
    s = lax.axis_index("s")
    x = lax.axis_index("x")
    yh = lax.axis_index("yh")
    z = lax.axis_index("z")
    c = lax.axis_index("c")
    diag = c == yh
    weights_in = (wq_in, wo_in, wu_in, wd_in)
    weights = (wq, wo, wu, wd)
    grads = (g0, g1, g2, g3)
    zrecv = (zr0, zr1, zr2, zr3)
    yout = (yo0, yo1, yo2, yo3)
    yrecv = (yr0, yr1, yr2, yr3)
    final = (f0, f1, f2, f3)
    outs = (gq, go, gu, gd)

    def at_piece(ref, k, zi, lead=()):
        rows = pl.ds(pl.multiple_of(zi * PIECE[k], PIECE[k]), PIECE[k])
        if k == QKV:
            return ref.at[(*lead, slice(None), rows)]
        return ref.at[(*lead, rows)]

    def y_dev(i):
        return {"s": lax.rem(s + i % 2, 2), "yh": lax.rem(yh + i // 2, 2)}

    def z_dev(d):
        return {"z": lax.rem(z + d, 4)}

    core = {"c": 1 - c}

    for i, ref in enumerate((ob_in, ga_in, sa_in, db_in, gb_in, sb_in)):
        sw_in[i : i + 1, :] = ref[...].astype(F32)
    sw_in[6:7, 0:512] = ub_in[...].astype(F32)
    sw_in[6:7, 512:640] = qb_in[0, 0:1, :].astype(F32)
    sw_in[6:7, 640:768] = qb_in[0, 1:2, :].astype(F32)
    for m in range(2):
        seg[m] = jnp.broadcast_to(seg_in[m], (8, SEQ))

    barrier = pltpu.get_barrier_semaphore()

    def greet(dev):
        pl.semaphore_signal(barrier, inc=1, device_id=dev, device_id_type=MESH)

    for d in (1, 2, 3):
        greet({"x": lax.rem(x + d, 4)})
        greet(z_dev(d))
        greet(y_dev(d))
    greet(core)

    @pl.when(diag)
    def _():
        pl.semaphore_wait(barrier, 10)

    @pl.when(jnp.logical_not(diag))
    def _():
        greet({"s": s, "yh": c, "c": yh})
        greet({"s": 1 - s, "yh": c, "c": yh})
        pl.semaphore_wait(barrier, 12)

    def rows_of(xi, h, ci):
        return pl.ds(pl.multiple_of(xi * 128 + h * BLK + ci * HALF, HALF), HALF)

    mirror = {"yh": c, "c": yh}
    swaps = (
        (inp.at[s, pl.ds(0, HALF)], hbuf.at[0, rows_of(x, 0, yh)]),
        (inp.at[s, pl.ds(HALF, HALF)], hbuf.at[0, rows_of(x, 1, yh)]),
        (seg.at[s], segb),
        (cot.at[s], cotb),
    )

    def swap_start(i):
        src, dst = swaps[i]

        @pl.when(diag)
        def _():
            pltpu.make_async_copy(src, dst, swap_r.at[i]).start()

        @pl.when(jnp.logical_not(diag))
        def _():
            remote(src, dst, swap_s.at[i], swap_r.at[i], mirror).start()

    def swap_wait(i):
        src, dst = swaps[i]

        @pl.when(diag)
        def _():
            pltpu.make_async_copy(src, dst, swap_r.at[i]).wait()

        @pl.when(jnp.logical_not(diag))
        def _():
            remote(src, dst, swap_s.at[i], swap_r.at[i], mirror).wait()

    def wy_copy(k, i, j):
        if k == 4:
            return remote(sw_in, sw.at[s], wy_s.at[k, i, j], wy_r.at[s, k, j], y_dev(i))
        zi = lax.rem(z + j, 4)
        src = at_piece(weights_in[k], k, zi)
        dst = at_piece(weights[k], k, zi, (s,))
        return remote(src, dst, wy_s.at[k, i, j], wy_r.at[s, k, j], y_dev(i))

    def wy_arrival(l, k, j):
        if k == 4:
            return remote(sw_in, sw.at[l], wy_s.at[k, 0, j], wy_r.at[l, k, j], core)
        dst = at_piece(weights[k], k, lax.rem(z + j, 4), (l,))
        return remote(dst, dst, wy_s.at[k, 0, j], wy_r.at[l, k, j], core)

    def wl_copy(k):
        if k == 4:
            return pltpu.make_async_copy(sw_in, sw.at[s], wl.at[k])
        return pltpu.make_async_copy(weights_in[k], weights[k].at[s], wl.at[k])

    def wz_copy(l, k, d):
        piece = at_piece(weights[k], k, lax.rem(z + d // 2, 4), (l,))
        return remote(piece, piece, wz_s.at[l, k, d], wz_r.at[l, k, d], z_dev(d))

    def wz_arrival(l, k, d):
        piece = at_piece(weights[k], k, lax.rem(z + (3 if d == 1 else 2), 4), (l,))
        return remote(piece, piece, wz_s.at[l, k, d], wz_r.at[l, k, d], z_dev(d))

    def mine(l):
        return jnp.logical_and(diag, s == l)

    def relay(l, k):
        @pl.when(jnp.logical_not(mine(l)))
        def _():
            wy_arrival(l, k, 0).wait_recv()
            if k != 4:
                wz_copy(l, k, 1).start()
                wy_arrival(l, k, 1).wait_recv()
                wz_copy(l, k, 3).start()

    def ready(l, k):
        @pl.when(mine(l))
        def _():
            wl_copy(k).wait()

        @pl.when(jnp.logical_not(mine(l)))
        def _():
            for d in (1, 3):
                wz_arrival(l, k, d).wait_recv()

    def spread(l, k):
        @pl.when(mine(l))
        def _():
            for j in range(1 if k == 4 else 2):
                for i in (1, 3, 2):
                    wy_copy(k, i, j).start()
            wl_copy(k).start()

    swap_start(0)
    swap_start(1)
    spread(0, 4)
    spread(0, QKV)
    spread(1, 4)
    swap_start(2)

    def arrival(i):
        return i + (i // 2) * (5 - 2 * i)

    def reversed_arrival(i):
        return arrival(3 - i)

    def ag_direct(ph, view, h, d):
        block = view.at[rows_of(x, h, c)]
        sem = 4 * h + d
        return remote(block, block, ag_s.at[ph, sem], ag_r.at[ph, sem], {"x": lax.rem(x + d, 4)})

    def ag_forward(ph, view, h, d):
        block = view.at[rows_of(lax.rem(x + 4 - d, 4), h, c)]
        return remote(block, block, cg_s.at[ph, 4 * h + d], cg_r.at[ph, 4 * h + d], core)

    def ag_start(ph, view, h):
        for d in (1, 3, 2):
            ag_direct(ph, view, h, d).start()
        ag_forward(ph, view, h, 0).start()

    def block_rows(h, d):
        return pl.ds(pl.multiple_of(lax.rem(x + 4 - d, 4) * 128 + h * BLK, BLK), BLK)

    def pair_rows(t, order):
        h = t // 2
        i = 2 * (t - 2 * h)
        return block_rows(h, order(i)), block_rows(h, order(i + 1))

    def load(ref, lead, pair):
        return jnp.concatenate([ref[(*lead, at, slice(None))] for at in pair], axis=0)

    def store(ref, lead, pair, value):
        for i, at in enumerate(pair):
            ref[(*lead, at, slice(None))] = value[i * BLK : (i + 1) * BLK]

    def ag_pair(ph, view, t):
        h = t // 2

        @pl.when(t == 2 * h)
        def _():
            for d in (1, 3):
                ag_direct(ph, view, h, d).wait_recv()
                ag_forward(ph, view, h, d).start()

        @pl.when(t != 2 * h)
        def _():
            ag_direct(ph, view, h, 2).wait_recv()
            ag_forward(ph, view, h, 2).start()

        i = 2 * (t - 2 * h)
        ag_forward(ph, view, h, arrival(i)).wait_recv()
        ag_forward(ph, view, h, arrival(i + 1)).wait_recv()
        return pair_rows(t, arrival)

    def ag_end(ph, view):
        for h in range(2):
            for d in (1, 2, 3):
                ag_direct(ph, view, h, d).wait_send()
            for d in range(4):
                ag_forward(ph, view, h, d).wait_send()

    my_half = pl.ds(pl.multiple_of(c * HALF, HALF), HALF)
    other_half = pl.ds(pl.multiple_of((1 - c) * HALF, HALF), HALF)

    def ra_copy(ph, slot):
        return remote(aout.at[slot], ain.at[ph, slot], ra_s.at[ph, slot], ra_r.at[ph, slot], core)

    def rb_copy(ph, slot):
        target = {"x": lax.rem(x + 8 - slot, 4)}
        return remote(bout.at[slot], bin_.at[ph, slot], rb_s.at[ph, slot], rb_r.at[ph, slot], target)

    def rs_begin(ph, slot, value):
        part[slot] = value
        aout[slot] = part[slot, other_half, :].astype(BF)
        ra_copy(ph, slot).start()

    def rs_pass(ph, h, d):
        slot = 4 * h + d
        ra_copy(ph, slot).wait_recv()
        total = part[slot, my_half, :] + ain[ph, slot].astype(F32)

        @pl.when(d == 0)
        def _():
            res[h] = total

        @pl.when(d != 0)
        def _():
            bout[slot] = total.astype(BF)
            rb_copy(ph, slot).start()

    def rs_loop(ph, order, step):
        def pass_pair(t):
            h = t // 2
            for i in range(2):
                rs_pass(ph, h, order(2 * (t - 2 * h) + i))

        def one(t, carry):
            h = t // 2
            value = step(t)
            for i in range(2):
                d = order(2 * (t - 2 * h) + i)
                rs_begin(ph, 4 * h + d, value[i * BLK : (i + 1) * BLK])

            @pl.when(t > 0)
            def _():
                pass_pair(t - 1)

            return carry

        lax.fori_loop(0, 4, one, 0)
        pass_pair(3)

    def rs_end(ph, h):
        total = res[h]
        for d in (1, 3, 2):
            slot = 4 * h + d
            rb_copy(ph, slot).wait_recv()
            total = total + bin_[ph, slot].astype(F32)
        for d in range(4):
            ra_copy(ph, 4 * h + d).wait_send()
        for d in (1, 2, 3):
            rb_copy(ph, 4 * h + d).wait_send()
        return total

    lanes = lax.broadcasted_iota(jnp.int32, (1, 128), 1) < 64
    head_mask = (
        lanes.astype(F32).astype(BF),
        (1.0 - lanes.astype(F32)).astype(BF),
    )
    first_head = lax.broadcasted_iota(jnp.int32, (128, 128), 1) < 64

    def home_copy(l, src, dst, send, recv):
        return remote(src.at[l], dst.at[s], send.at[l], recv.at[s], {"s": l, "yh": c, "c": yh})

    def home_start(l, src, dst, send, recv):
        @pl.when(mine(l))
        def _():
            dst[s] = src[l]

        @pl.when(jnp.logical_not(mine(l)))
        def _():
            home_copy(l, src, dst, send, recv).start()

    def home_wait(src, dst, send, recv):
        for l in range(2):
            @pl.when(jnp.logical_not(mine(l)))
            def _():
                home_copy(l, src, dst, send, recv).wait_send()
                remote(src.at[l], dst.at[l], send.at[l], recv.at[l], core).wait_recv()

    for h in range(2):
        swap_wait(h)
        ag_start(FA, hbuf.at[0], h)
    relay(0, 4)
    swap_wait(2)
    documents = lax.broadcasted_iota(jnp.int32, (8, SEQ), 0) == segb[...]
    documents = documents.astype(F32).astype(BF)
    put = lax.broadcasted_iota(jnp.int32, (SEQ, SEQ), 1)
    put = put - lax.rem(put, 128) + lax.rem(put, 64) // 32 * 64 + lax.rem(put, 128) // 64 * 32 + lax.rem(put, 32)
    move = lax.broadcasted_iota(jnp.int32, (SEQ, SEQ), 0) == put
    documents = dot_nn(documents, move.astype(F32).astype(BF)).astype(BF)
    bias[...] = jnp.where(dot_tn(documents, documents) > 0.5, 0.0, -1e30)
    relay(0, QKV)
    spread(0, OUT)
    spread(0, UP)
    spread(0, DOWN)
    relay(1, 4)

    @pl.when(diag)
    def _():
        wl_copy(4).wait()

    def forward(l, carry):
        small = sw[l]
        out_b, gain_a, shift_a = small[0:1], small[1:2], small[2:3]
        down_b, gain_b, shift_b = small[3:4], small[4:5], small[5:6]
        view = hbuf.at[l]
        ready(l, QKV)

        def project(t, carry):
            at = ag_pair(FA, view, t)
            rows = load(hbuf, (l,), at)
            q = dot_nn(rows, wq[l, 0]) + sw[l, 6:7, 512:640]
            k = dot_nn(rows, wq[l, 1])
            v = dot_nn(rows, wq[l, 2]) + sw[l, 6:7, 640:768]
            store(qkv, (l, 0), at, q.astype(BF))
            store(qkv, (l, 1), at, k.astype(BF))
            store(qkv, (l, 2), at, v.astype(BF))
            return carry

        lax.fori_loop(0, 4, project, 0)

        @pl.when(l == 1)
        def _():
            relay(1, UP)
            relay(1, DOWN)


        @pl.when(l == 0)
        def _():
            relay(0, OUT)

        ready(l, OUT)

        def attend(t):
            @pl.when(jnp.logical_and(l == 0, t == 1))
            def _():
                for k in (QKV, OUT, UP, DOWN):
                    spread(1, k)

            @pl.when(jnp.logical_and(l == 0, t == 2))
            def _():
                relay(0, UP)

            at = pair_rows(t, reversed_arrival)
            q = load(qkv, (l, 0), at)
            mask = load(bias, (), at)
            keys = qkv[l, 1]
            values = qkv[l, 2]
            heads = []
            for j in range(2):
                scores = dot_nt(q * head_mask[j], keys) * 0.125 + mask
                e = jnp.exp(scores - jnp.max(scores, axis=-1, keepdims=True))
                p = (e * (1.0 / jnp.sum(e, axis=-1, keepdims=True))).astype(BF)
                store(probs, (l, j), at, p)
                heads.append(dot_nn(p, values))
            block = jnp.where(first_head, heads[0], heads[1]).astype(BF)
            store(att, (l,), at, block)
            return dot_nn(block, wo[l])

        rs_loop(FA, reversed_arrival, attend)

        @pl.when(l == 0)
        def _():
            relay(0, DOWN)

        ar_view = arbuf.at[l]
        for h in range(2):
            r1 = hbuf[l, rows_of(x, h, c), :].astype(F32) + rs_end(FA, h) + out_b
            n, scale = normed(r1)
            n1[l, h] = n
            sc1[l, h] = jnp.broadcast_to(scale, (HALF, 128))
            a = n * gain_a + shift_a
            abuf[h] = a
            arbuf[l, rows_of(x, h, c), :] = a.astype(BF)
            ag_start(FM, ar_view, h)
        ag_end(FA, view)
        ready(l, UP)
        ready(l, DOWN)

        def feed(t):
            @pl.when(jnp.logical_and(l == 0, t == 3))
            def _():
                relay(1, QKV)

            at = ag_pair(FM, ar_view, t)
            u = dot_nn(load(arbuf, (l,), at), wu[l]) + sw[l, 6:7, 0:512]
            cdf = 0.5 * (1.0 + lax.erf(u * 0.7071067811865476))
            store(gp, (l,), at, cdf + u * (jnp.exp(-0.5 * u * u) * 0.3989422804014327))
            g = (u * cdf).astype(BF)
            store(gr, (l,), at, g)
            return dot_nn(g, wd[l])

        rs_loop(FM, arrival, feed)
        for h in range(2):
            r2 = abuf[h] + rs_end(FM, h) + down_b
            n, scale = normed(r2)
            n2[l, h] = n
            sc2[l, h] = jnp.broadcast_to(scale, (HALF, 128))
            y = (n * gain_b + shift_b).astype(BF)
            yb[l, h * HALF : (h + 1) * HALF, :] = y

            @pl.when(l == 0)
            def _():
                hbuf[1, rows_of(x, h, c), :] = y
                ag_start(FA, hbuf.at[1], h)

        ag_end(FM, ar_view)

        @pl.when(l == 0)
        def _():
            relay(1, OUT)
            swap_start(3)

        home_start(l, yb, lob, lo_s, lo_r)
        return carry

    lax.fori_loop(0, 2, forward, 0)

    def gz_copy(l, k, d):
        src = at_piece(grads[k], k, lax.rem(z + d, 4), (l,))
        return remote(src, zrecv[k].at[l, d - 1], gz_s.at[l, k, d], gz_r.at[l, k, d], z_dev(d))

    def gz_start(l, k):
        for d in (1, 3, 2):
            gz_copy(l, k, d).start()

    def gy_copy(l, k):
        slot = 2 * lax.rem(yh + 2 - c, 2) + lax.rem(s + 2 - l, 2)
        return remote(
            yout[k].at[l], yrecv[k].at[slot - 1], gy_s.at[l, k], gy_r.at[k, slot], {"s": l, "yh": c}
        )

    def gy_start(l, k):
        total = at_piece(grads[k], k, z, (l,))[...].astype(F32)
        for d in (1, 3, 2):
            gz_copy(l, k, d).wait_recv()
            total = total + zrecv[k][l, d - 1].astype(F32)
        yout[k][l] = total.astype(BF)

        @pl.when(jnp.logical_not(mine(l)))
        def _():
            gy_copy(l, k).start()

    def fz_copy(k, d):
        piece = at_piece(final[k], k, z)
        return remote(piece, piece, fz_s.at[k, d], fz_r.at[k, d], z_dev(d))

    def fc_copy(k, d):
        piece = at_piece(final[k], k, lax.rem(z + 4 - d, 4))
        return remote(piece, piece, fc_s.at[k, d], fc_r.at[k, d], core)

    def fz_start(k):
        @pl.when(diag)
        def _():
            total = yout[k][s].astype(F32)
            for i in (1, 2, 3):
                remote(
                    yrecv[k].at[i - 1], yrecv[k].at[i - 1], gy_s.at[0, k], gy_r.at[k, i], core
                ).wait_recv()
                total = total + yrecv[k][i - 1].astype(F32)
            at_piece(final[k], k, z)[...] = total.astype(BF)
            for d in (1, 3, 2):
                fz_copy(k, d).start()
            fc_copy(k, 0).start()

    def fc_start(k):
        @pl.when(diag)
        def _():
            for d in (1, 3, 2):
                piece = at_piece(final[k], k, lax.rem(z + 4 - d, 4))
                remote(piece, piece, fz_s.at[k, d], fz_r.at[k, d], z_dev(d)).wait_recv()
                fc_copy(k, d).start()

    def out_start(k):
        @pl.when(jnp.logical_not(diag))
        def _():
            for d in range(4):
                fc_copy(k, d).wait_recv()

        pltpu.make_async_copy(final[k], outs[k], st.at[k]).start()

    def sx_copy(l, d):
        return remote(gsb.at[l], sx.at[l, x], sx_s.at[l, d], sx_r.at[l, d], {"x": lax.rem(x + d, 4)})

    def sc_copy(l):
        return remote(sc.at[l, c], sc.at[l, c], sc_s.at[l], sc_r.at[l], core)

    def sz_copy(l, d):
        return remote(sz.at[l, z], sz.at[l, z], sz_s.at[l, d], sz_r.at[l, d], z_dev(d))

    def sy_copy(l, i):
        block = sy.at[l, 2 * yh + s]
        return remote(block, block, sy_s.at[l, i], sy_r.at[l, i], y_dev(i))

    def small_x(l):
        sx[l, x] = gsb[l]
        for d in (1, 3, 2):
            sx_copy(l, d).start()

    def small_core(l):
        for d in (1, 3, 2):
            sx_copy(l, d).wait_recv()
        sc[l, c] = ((sx[l, 0] + sx[l, 1]) + sx[l, 2]) + sx[l, 3]
        sc[l, c, 6:7, :] = gsb[l, 6:7, :]
        sc_copy(l).start()

    def small_z(l):
        sc_copy(l).wait_recv()
        sz[l, z] = sc[l, 0] + sc[l, 1]
        sz[l, z, 6:7, :] = sc[l, 0, 6:7, :]
        sz[l, z, 7:8, :] = sc[l, 1, 6:7, :]
        for d in (1, 3, 2):
            sz_copy(l, d).start()

    def small_y(l):
        for d in (1, 3, 2):
            sz_copy(l, d).wait_recv()
        sy[l, 2 * yh + s] = ((sz[l, 0] + sz[l, 1]) + sz[l, 2]) + sz[l, 3]
        for i in (1, 3, 2):
            sy_copy(l, i).start()

    def small_end():
        for l in range(2):
            for i in (1, 3, 2):
                sy_copy(l, i).wait_recv()
        gsout[...] = ((sy[s, 0] + sy[s, 1]) + sy[s, 2]) + sy[s, 3]

        @pl.when(yh == 1)
        def _():
            gsout[6:7, :] = gsout[7:8, :]

    swap_wait(3)

    def input_grad(l, h):
        low = (abuf[h] + rs_end(BA, h)).astype(BF)
        dhb[l, h * HALF : (h + 1) * HALF, :] = low
        return low.astype(F32)

    def grads_qkv(l):
        def some(i, carry):
            cols = pl.ds(pl.multiple_of(i * 128, 128), 128)
            rows = hbuf[l, :, cols]
            for j in range(3):
                g0[l, j, cols, :] = dot_tn(rows, dx[j]).astype(BF)
            return carry

        lax.fori_loop(0, 8, some, 0)
        gz_start(l, QKV)

    def grads_out(l):
        g1[l] = dot_tn(att[l], dprbuf[...]).astype(BF)
        gz_start(l, OUT)

    def grads_down(l):
        def some(i, carry):
            cols = pl.ds(pl.multiple_of(i * 128, 128), 128)
            g3[l, cols, :] = dot_tn(gr[l, :, cols], dmbuf[...]).astype(BF)
            return carry

        lax.fori_loop(0, 4, some, 0)
        gz_start(l, DOWN)

    def grads_up(l):
        def some(i, carry):
            cols = pl.ds(pl.multiple_of(i * 128, 128), 128)
            g2[l, cols, :] = dot_tn(arbuf[l, :, cols], dur[...]).astype(BF)
            return carry

        lax.fori_loop(0, 8, some, 0)
        gz_start(l, UP)

    def backward(step_index, carry):
        l = 1 - step_index
        small = sw[l]
        gain_a, gain_b = small[1:2], small[4:5]
        gsb[l] = jnp.zeros((8, D), F32)
        for h in range(2):
            @pl.when(l == 1)
            def _():
                dyb[...] = cotb[h * HALF : (h + 1) * HALF, :].astype(F32)

            @pl.when(l == 0)
            def _():
                dyb[...] = input_grad(1, h)

            dy = dyb[...]
            n = n2[l, h]
            dr2 = norm_back(dy, gain_b, n, sc2[l, h, :, 0:1])
            dmbuf[rows_of(x, h, c), :] = dr2.astype(BF)
            ag_start(BM, dmbuf, h)
            abuf[h] = dr2
            gsb[l, 4:5, :] += col_sum(dy * n)
            gsb[l, 5:6, :] += col_sum(dy)
            gsb[l, 3:4, :] += col_sum(dr2)

            @pl.when(l == 0)
            def _():
                if h == 0:
                    grads_qkv(1)
                else:
                    grads_out(1)
                    small_z(1)
                    ag_end(BA, dprbuf)
                    home_start(1, dhb, igb, ig_s, ig_r)

        def feed_back(t):
            at = ag_pair(BM, dmbuf, t)
            dg = dot_nt(load(dmbuf, (), at), wd[l])
            du = dg * load(gp, (l,), at)
            gsb[l, 6:7, 0:512] += col_sum(du)
            low = du.astype(BF)
            store(dur, (), at, low)
            return dot_nt(low, wu[l])

        rs_loop(BM, arrival, feed_back)
        for h in range(2):
            da = abuf[h] + rs_end(BM, h)
            n = n1[l, h]
            dr1 = norm_back(da, gain_a, n, sc1[l, h, :, 0:1])
            dprbuf[rows_of(x, h, c), :] = dr1.astype(BF)
            ag_start(BA, dprbuf, h)
            abuf[h] = dr1
            gsb[l, 1:2, :] += col_sum(da * n)
            gsb[l, 2:3, :] += col_sum(da)
            gsb[l, 0:1, :] += col_sum(dr1)
            if h == 0:
                grads_down(l)
            else:
                grads_up(l)
        ag_end(BM, dmbuf)
        dacc[...] = jnp.zeros_like(dacc)

        @pl.when(l == 0)
        def _():
            small_y(1)
            for k in (DOWN, UP):
                gy_start(1, k)

        def attend_back(t, carry):
            at = ag_pair(BA, dprbuf, t)
            grad = dot_nt(load(dprbuf, (), at), wo[l]).astype(BF)
            q = load(qkv, (l, 0), at)
            keys = qkv[l, 1]
            values = qkv[l, 2]
            heads = []
            dk = dacc[0]
            dv = dacc[1]
            for j in range(2):
                own = grad * head_mask[j]
                low_p = load(probs, (l, j), at)
                p = low_p.astype(F32)
                dp = dot_nt(own, values)
                ds = (p * (dp - jnp.sum(p * dp, axis=-1, keepdims=True))).astype(BF)
                heads.append(dot_nn(ds, keys))
                dk = dk + dot_tn(ds, q * head_mask[j])
                dv = dv + dot_tn(low_p, own)
            dacc[0] = dk
            dacc[1] = dv
            dq = (jnp.where(first_head, heads[0], heads[1]) * 0.125).astype(BF)
            store(dx, (0,), at, dq)
            gsb[l, 6:7, 512:640] += col_sum(dq.astype(F32))
            return carry

        lax.fori_loop(0, 4, attend_back, 0)
        dx[1] = (dacc[0] * 0.125).astype(BF)
        dv = dacc[1].astype(BF)
        dx[2] = dv
        gsb[l, 6:7, 640:768] = col_sum(dv.astype(F32))
        small_x(l)

        @pl.when(l == 0)
        def _():
            grads_qkv(0)
            grads_out(0)
            for k in (QKV, OUT):
                gy_start(1, k)

        def input_back(t):
            at = pair_rows(t, reversed_arrival)
            return (
                dot_nt(load(dx, (0,), at), wq[l, 0])
                + dot_nt(load(dx, (1,), at), wq[l, 1])
                + dot_nt(load(dx, (2,), at), wq[l, 2])
            )

        rs_loop(BA, reversed_arrival, input_back)
        small_core(l)
        return carry

    lax.fori_loop(0, 2, backward, 0)
    for k in (DOWN, UP):
        gy_start(0, k)
    small_z(0)
    for h in range(2):
        input_grad(0, h)
    ag_end(BA, dprbuf)
    home_start(0, dhb, igb, ig_s, ig_r)
    small_y(0)

    for k in (DOWN, UP):
        fz_start(k)
    for k in (QKV, OUT):
        gy_start(0, k)
    for k in (DOWN, UP):
        fc_start(k)
    for k in (QKV, OUT):
        fz_start(k)
    home_wait(yb, lob, lo_s, lo_r)
    lo_out = pltpu.make_async_copy(lob, lo, st.at[5])
    lo_out.start()
    home_wait(dhb, igb, ig_s, ig_r)
    ig_out = pltpu.make_async_copy(igb, ig, st.at[6])
    ig_out.start()
    small_end()
    small_out = pltpu.make_async_copy(gsout, gs, st.at[4])
    small_out.start()
    for k in (DOWN, UP):
        out_start(k)
    for k in (QKV, OUT):
        fc_start(k)
    for k in (QKV, OUT):
        out_start(k)

    @pl.when(diag)
    def _():
        for k in range(5):
            for i in (1, 2, 3):
                for j in range(1 if k == 4 else 2):
                    wy_copy(k, i, j).wait_send()

    for l in range(2):
        for k in range(4):
            @pl.when(jnp.logical_not(mine(l)))
            def _():
                for d in (1, 3):
                    wz_copy(l, k, d).wait_send()
                gy_copy(l, k).wait_send()

            for d in (1, 2, 3):
                gz_copy(l, k, d).wait_send()

        for d in (1, 2, 3):
            sx_copy(l, d).wait_send()
            sz_copy(l, d).wait_send()
            sy_copy(l, d).wait_send()
        sc_copy(l).wait_send()

    @pl.when(diag)
    def _():
        for k in range(4):
            for d in (1, 2, 3):
                fz_copy(k, d).wait_send()
            for d in range(4):
                fc_copy(k, d).wait_send()

    small_out.wait()
    lo_out.wait()
    ig_out.wait()
    for k in range(4):
        pltpu.make_async_copy(final[k], outs[k], st.at[k]).wait()


WSHAPES = ((3, D, 128), (128, D), (D, FFS), (FFS, D))
PSHAPES = ((3, 256, 128), (32, D), (256, FFS), (128, D))


def run(*operands):
    vm = pltpu.VMEM
    scratch = [vm((8, D), F32), vm((2, 8, SEQ), jnp.int32)]
    scratch += [vm((2, *shape), BF) for shape in WSHAPES]
    scratch += [vm((2, 8, D), F32)]
    scratch += [vm((2, SEQ, D), BF)] * 2 + [vm((SEQ, D), BF)] * 2
    scratch += [vm((4, 8, HALF, D), BF)] * 2 + [vm((8, HALF, D), BF)] * 2 + [vm((8, BLK, D), F32)]
    scratch += [
        vm((2, 3, SEQ, 128), BF),
        vm((2, SEQ, 128), BF),
        vm((2, 2, SEQ, SEQ), BF),
        vm((2, SEQ, FFS), F32),
        vm((2, SEQ, FFS), BF),
        vm((2, 2, HALF, D), F32),
        vm((2, 2, HALF, D), F32),
        vm((2, 2, HALF, 128), F32),
        vm((2, 2, HALF, 128), F32),
        vm((2, HALF, D), F32),
        vm((2, HALF, D), F32),
        vm((HALF, D), F32),
    ]
    scratch += [
        vm((8, SEQ), jnp.int32),
        vm((SEQ, SEQ), F32),
        vm((BLK, D), BF),
        vm((SEQ, FFS), BF),
        vm((2, SEQ, 128), F32),
        vm((3, SEQ, 128), BF),
    ]
    scratch += [vm((2, BLK, D), BF)] * 4 + [vm((2, 8, D), F32)]
    scratch += [vm((2, n, 8, D), F32) for n in (4, 2, 4, 4)] + [vm((8, D), F32)]
    scratch += [vm((2, *shape), BF) for shape in WSHAPES]
    scratch += [vm((2, 3, *shape), BF) for shape in PSHAPES]
    scratch += [vm((2, *shape), BF) for shape in PSHAPES]
    scratch += [vm((3, *shape), BF) for shape in PSHAPES]
    scratch += [vm(shape, BF) for shape in WSHAPES]
    dma = pltpu.SemaphoreType.DMA
    scratch += [dma((4,)), dma((4,)), dma((5, 4, 2)), dma((2, 5, 2)), dma((2, 4, 4)), dma((2, 4, 4)), dma((5,))]
    scratch += [dma((4, 8))] * 8
    scratch += [dma((2,))] * 4
    scratch += [dma((2, 4, 4)), dma((2, 4, 4)), dma((2, 4)), dma((4, 4))]
    scratch += [dma((4, 4))] * 4 + [dma((7,))]
    scratch += [dma((2, 4))] * 2 + [dma((2,))] * 2 + [dma((2, 4))] * 4
    any_space = pl.BlockSpec(memory_space=pl.ANY)
    in_vmem = pl.BlockSpec(memory_space=pltpu.VMEM)
    return pl.pallas_call(
        kernel,
        out_shape=[
            jax.ShapeDtypeStruct((2, BLK, D), BF),
            jax.ShapeDtypeStruct((2, BLK, D), BF),
            *(jax.ShapeDtypeStruct(shape, BF) for shape in WSHAPES),
            jax.ShapeDtypeStruct((8, D), F32),
        ],
        in_specs=[any_space] * 2 + [in_vmem] + [any_space] * 4 + [in_vmem] * 8,
        out_specs=[any_space] * 7,
        scratch_shapes=scratch,
        compiler_params=pltpu.CompilerParams(
            collective_id=0, has_side_effects=True, vmem_limit_bytes=60 * 1024 * 1024
        ),
    )(*operands)


def finish_kernel(lo, ig, gq, go, gu, gd, gs, lo_o, ig_o, gq_o, qv_o, go_o, ob_o, ga_o, sa_o, gu_o, ub_o, gd_o, db_o, gb_o, sb_o):
    lo_o[0, :, 0] = lo[...]
    ig_o[0, :, 0] = ig[...]
    gq_o[0] = gq[...].astype(F32)
    go_o[0] = go[...].astype(F32)
    gu_o[0] = gu[...].astype(F32)
    gd_o[0] = gd[...].astype(F32)
    for row, ref in enumerate((ob_o, ga_o, sa_o, db_o, gb_o, sb_o)):
        ref[...] = gs[row : row + 1, :]
    ub_o[...] = gs[6:7, 0:512]
    qv_o[0, 0:1, :] = gs[6:7, 512:640]
    qv_o[0, 1:2, :] = gs[6:7, 640:768]


FSHAPES = ((3, 512, 128), (64, D), (512, FFS), (256, D))


def finish(lo, ig, *rest):
    steps = 2
    row = ((1, D), lambda i: (0, 0))
    wide = ((2, BLK // steps, D), lambda i: (0, i, 0))
    wide_out = ((1, 2, 1, BLK // steps, D), lambda i: (0, 0, 0, i, 0))
    wmaps = ((lambda i: (0, i, 0)), (lambda i: (i, 0)), (lambda i: (i, 0)), (lambda i: (i, 0)))
    omaps = ((lambda i: (0, 0, i, 0)),) + ((lambda i: (0, i, 0)),) * 3
    gq_o, go_o, gu_o, gd_o = (((1, *shape), m) for shape, m in zip(FSHAPES, omaps))
    specs_in = [wide, wide, *zip(FSHAPES, wmaps), ((8, D), lambda i: (0, 0))]
    specs_out = [
        wide_out, wide_out, gq_o, ((1, 2, 128), lambda i: (0, 0, 0)), go_o, row, row, row,
        gu_o, ((1, FFS), lambda i: (0, 0)), gd_o, row, row, row,
    ]
    full = [
        ((1, 2, 1, BLK, D), BF), ((1, 2, 1, BLK, D), BF), ((1, 3, D, 128), F32), ((1, 2, 128), F32),
        ((1, 128, D), F32), ((1, D), F32), ((1, D), F32), ((1, D), F32), ((1, D, FFS), F32),
        ((1, FFS), F32), ((1, FFS, D), F32), ((1, D), F32), ((1, D), F32), ((1, D), F32),
    ]
    return pl.pallas_call(
        finish_kernel,
        grid=(steps,),
        out_shape=[jax.ShapeDtypeStruct(*leaf) for leaf in full],
        in_specs=[pl.BlockSpec(*spec) for spec in specs_in],
        out_specs=[pl.BlockSpec(*spec) for spec in specs_out],
        compiler_params=pltpu.CompilerParams(vmem_limit_bytes=60 * 1024 * 1024),
    )(lo, ig, *rest)


def local(
    inputs, segments, qkv_weight, qv_bias, out_weight, out_bias, gain_one, shift_one,
    up_weight, up_bias, down_weight, down_bias, gain_two, shift_two, cotangent,
):
    results = run(
        inputs[:, 0], cotangent[:, 0], segments,
        qkv_weight[0], out_weight[0], up_weight[0], down_weight[0],
        out_bias, gain_one, shift_one, down_bias, gain_two, shift_two, up_bias, qv_bias,
    )
    return tuple(finish(*results))


def solution(mesh):
    fine = Mesh(mesh.devices.reshape(2, 4, 2, 4, 2), ("s", "x", "yh", "z", "c"))
    t = ("x", "yh")
    dp = ("z", "c")
    return jax.shard_map(
        local,
        mesh=fine,
        in_specs=(
            P(None, dp, t, None),
            P(None, dp, None),
            P("s", None, None, t),
            P("s", None, t),
            P("s", t, None),
            P("s", None),
            P("s", None),
            P("s", None),
            P("s", None, t),
            P("s", t),
            P("s", t, None),
            P("s", None),
            P("s", None),
            P("s", None),
            P(None, dp, t, None),
        ),
        out_specs=(
            P("s", None, dp, t, None),
            P("s", None, dp, t, None),
            P("s", None, None, t),
            P("s", None, t),
            P("s", t, None),
            P("s", None),
            P("s", None),
            P("s", None),
            P("s", None, t),
            P("s", t),
            P("s", t, None),
            P("s", None),
            P("s", None),
            P("s", None),
        ),
        check_vma=False,
    )
```

```python
import jax
import jax.numpy as jnp
from jax import lax
from jax.experimental import pallas as pl
from jax.experimental.pallas import tpu as pltpu
from jax.sharding import Mesh
from jax.sharding import PartitionSpec as P


BF = jnp.bfloat16
F32 = jnp.float32
MESH = pl.DeviceIdType.MESH
D = 1024
FFS = 512
SEQ = 512
BLK = 64
HALF = 32
QKV, OUT, UP, DOWN = 0, 1, 2, 3
PIECE = (256, 32, 256, 128)
FA, FM, BM, BA = 0, 1, 2, 3


def remote(src, dst, send, recv, dev):
    return pltpu.make_async_remote_copy(
        src_ref=src, dst_ref=dst, send_sem=send, recv_sem=recv, device_id=dev, device_id_type=MESH
    )


def dot_nn(a, b):
    return lax.dot_general(a, b, (((1,), (0,)), ((), ())), preferred_element_type=F32)


def dot_nt(a, b):
    return lax.dot_general(a, b, (((1,), (1,)), ((), ())), preferred_element_type=F32)


def dot_tn(a, b):
    return lax.dot_general(a, b, (((0,), (0,)), ((), ())), preferred_element_type=F32)


def normed(r):
    center = r - jnp.mean(r, axis=-1, keepdims=True)
    scale = lax.rsqrt(jnp.mean(center * center, axis=-1, keepdims=True) + 1e-06)
    return center * scale, scale


def norm_back(dy, gain, n, scale):
    e = dy * gain
    mean_e = jnp.mean(e, axis=-1, keepdims=True)
    mean_en = jnp.mean(e * n, axis=-1, keepdims=True)
    return (e - mean_e - n * mean_en) * scale


def col_sum(v):
    return jnp.sum(v, axis=0, keepdims=True)


def kernel(
    inp, cot, seg_in, wq_in, wo_in, wu_in, wd_in,
    ob_in, ga_in, sa_in, db_in, gb_in, sb_in, ub_in, qb_in,
    lo, ig, gq, go, gu, gd, gs,
    sw_in, seg,
    wq, wo, wu, wd, sw,
    hbuf, arbuf, dmbuf, dprbuf,
    ain, bin_, aout, bout, part,
    qkv, att, probs, gp, gr, n1, n2, sc1, sc2, abuf, res, dyb,
    segb, bias, cotb, dur, dacc, dx,
    yb, lob, dhb, igb, gsb, sx, sc, sz, sy, gsout,
    g0, g1, g2, g3,
    zr0, zr1, zr2, zr3,
    yo0, yo1, yo2, yo3,
    yr0, yr1, yr2, yr3,
    f0, f1, f2, f3,
    swap_s, swap_r, wy_s, wy_r, wz_s, wz_r, wl,
    ag_s, ag_r, cg_s, cg_r, ra_s, ra_r, rb_s, rb_r,
    lo_s, lo_r, ig_s, ig_r,
    gz_s, gz_r, gy_s, gy_r, fz_s, fz_r, fc_s, fc_r, st, sx_s, sx_r, sc_s, sc_r, sz_s, sz_r, sy_s, sy_r,
):
    s = lax.axis_index("s")
    x = lax.axis_index("x")
    yh = lax.axis_index("yh")
    z = lax.axis_index("z")
    c = lax.axis_index("c")
    diag = c == yh
    weights_in = (wq_in, wo_in, wu_in, wd_in)
    weights = (wq, wo, wu, wd)
    grads = (g0, g1, g2, g3)
    zrecv = (zr0, zr1, zr2, zr3)
    yout = (yo0, yo1, yo2, yo3)
    yrecv = (yr0, yr1, yr2, yr3)
    final = (f0, f1, f2, f3)
    outs = (gq, go, gu, gd)

    def at_piece(ref, k, zi, lead=()):
        rows = pl.ds(pl.multiple_of(zi * PIECE[k], PIECE[k]), PIECE[k])
        if k == QKV:
            return ref.at[(*lead, slice(None), rows)]
        return ref.at[(*lead, rows)]

    def y_dev(i):
        return {"s": lax.rem(s + i % 2, 2), "yh": lax.rem(yh + i // 2, 2)}

    def z_dev(d):
        return {"z": lax.rem(z + d, 4)}

    core = {"c": 1 - c}

    for i, ref in enumerate((ob_in, ga_in, sa_in, db_in, gb_in, sb_in)):
        sw_in[i : i + 1, :] = ref[...].astype(F32)
    sw_in[6:7, 0:512] = ub_in[...].astype(F32)
    sw_in[6:7, 512:640] = qb_in[0, 0:1, :].astype(F32)
    sw_in[6:7, 640:768] = qb_in[0, 1:2, :].astype(F32)
    for m in range(2):
        seg[m] = jnp.broadcast_to(seg_in[m], (8, SEQ))

    barrier = pltpu.get_barrier_semaphore()

    def greet(dev):
        pl.semaphore_signal(barrier, inc=1, device_id=dev, device_id_type=MESH)

    for d in (1, 2, 3):
        greet({"x": lax.rem(x + d, 4)})
        greet(z_dev(d))
        greet(y_dev(d))
    greet(core)

    @pl.when(diag)
    def _():
        pl.semaphore_wait(barrier, 10)

    @pl.when(jnp.logical_not(diag))
    def _():
        greet({"s": s, "yh": c, "c": yh})
        greet({"s": 1 - s, "yh": c, "c": yh})
        pl.semaphore_wait(barrier, 12)

    def rows_of(xi, h, ci):
        return pl.ds(pl.multiple_of(xi * 128 + h * BLK + ci * HALF, HALF), HALF)

    mirror = {"yh": c, "c": yh}
    swaps = (
        (inp.at[s, pl.ds(0, HALF)], hbuf.at[0, rows_of(x, 0, yh)]),
        (inp.at[s, pl.ds(HALF, HALF)], hbuf.at[0, rows_of(x, 1, yh)]),
        (seg.at[s], segb),
        (cot.at[s], cotb),
    )

    def swap_start(i):
        src, dst = swaps[i]

        @pl.when(diag)
        def _():
            pltpu.make_async_copy(src, dst, swap_r.at[i]).start()

        @pl.when(jnp.logical_not(diag))
        def _():
            remote(src, dst, swap_s.at[i], swap_r.at[i], mirror).start()

    def swap_wait(i):
        src, dst = swaps[i]

        @pl.when(diag)
        def _():
            pltpu.make_async_copy(src, dst, swap_r.at[i]).wait()

        @pl.when(jnp.logical_not(diag))
        def _():
            remote(src, dst, swap_s.at[i], swap_r.at[i], mirror).wait()

    def wy_copy(k, i, j):
        if k == 4:
            return remote(sw_in, sw.at[s], wy_s.at[k, i, j], wy_r.at[s, k, j], y_dev(i))
        zi = lax.rem(z + j, 4)
        src = at_piece(weights_in[k], k, zi)
        dst = at_piece(weights[k], k, zi, (s,))
        return remote(src, dst, wy_s.at[k, i, j], wy_r.at[s, k, j], y_dev(i))

    def wy_arrival(l, k, j):
        if k == 4:
            return remote(sw_in, sw.at[l], wy_s.at[k, 0, j], wy_r.at[l, k, j], core)
        dst = at_piece(weights[k], k, lax.rem(z + j, 4), (l,))
        return remote(dst, dst, wy_s.at[k, 0, j], wy_r.at[l, k, j], core)

    def wl_copy(k):
        if k == 4:
            return pltpu.make_async_copy(sw_in, sw.at[s], wl.at[k])
        return pltpu.make_async_copy(weights_in[k], weights[k].at[s], wl.at[k])

    def wz_copy(l, k, d):
        piece = at_piece(weights[k], k, lax.rem(z + d // 2, 4), (l,))
        return remote(piece, piece, wz_s.at[l, k, d], wz_r.at[l, k, d], z_dev(d))

    def wz_arrival(l, k, d):
        piece = at_piece(weights[k], k, lax.rem(z + (3 if d == 1 else 2), 4), (l,))
        return remote(piece, piece, wz_s.at[l, k, d], wz_r.at[l, k, d], z_dev(d))

    def mine(l):
        return jnp.logical_and(diag, s == l)

    def relay(l, k):
        @pl.when(jnp.logical_not(mine(l)))
        def _():
            wy_arrival(l, k, 0).wait_recv()
            if k != 4:
                wz_copy(l, k, 1).start()
                wy_arrival(l, k, 1).wait_recv()
                wz_copy(l, k, 3).start()

    def ready(l, k):
        @pl.when(mine(l))
        def _():
            wl_copy(k).wait()

        @pl.when(jnp.logical_not(mine(l)))
        def _():
            for d in (1, 3):
                wz_arrival(l, k, d).wait_recv()

    def spread(l, k):
        @pl.when(mine(l))
        def _():
            for j in range(1 if k == 4 else 2):
                for i in (1, 3, 2):
                    wy_copy(k, i, j).start()
            wl_copy(k).start()

    swap_start(0)
    swap_start(1)
    spread(0, 4)
    spread(0, QKV)
    spread(1, 4)
    swap_start(2)

    def arrival(i):
        return i + (i // 2) * (5 - 2 * i)

    def reversed_arrival(i):
        return arrival(3 - i)

    def ag_direct(ph, view, h, d):
        block = view.at[rows_of(x, h, c)]
        sem = 4 * h + d
        return remote(block, block, ag_s.at[ph, sem], ag_r.at[ph, sem], {"x": lax.rem(x + d, 4)})

    def ag_forward(ph, view, h, d):
        block = view.at[rows_of(lax.rem(x + 4 - d, 4), h, c)]
        return remote(block, block, cg_s.at[ph, 4 * h + d], cg_r.at[ph, 4 * h + d], core)

    def ag_start(ph, view, h):
        for d in (1, 3, 2):
            ag_direct(ph, view, h, d).start()
        ag_forward(ph, view, h, 0).start()

    def block_rows(h, d):
        return pl.ds(pl.multiple_of(lax.rem(x + 4 - d, 4) * 128 + h * BLK, BLK), BLK)

    def pair_rows(t, order):
        h = t // 2
        i = 2 * (t - 2 * h)
        return block_rows(h, order(i)), block_rows(h, order(i + 1))

    def load(ref, lead, pair):
        return jnp.concatenate([ref[(*lead, at, slice(None))] for at in pair], axis=0)

    def store(ref, lead, pair, value):
        for i, at in enumerate(pair):
            ref[(*lead, at, slice(None))] = value[i * BLK : (i + 1) * BLK]

    def ag_pair(ph, view, t):
        h = t // 2

        @pl.when(t == 2 * h)
        def _():
            for d in (1, 3):
                ag_direct(ph, view, h, d).wait_recv()
                ag_forward(ph, view, h, d).start()

        @pl.when(t != 2 * h)
        def _():
            ag_direct(ph, view, h, 2).wait_recv()
            ag_forward(ph, view, h, 2).start()

        i = 2 * (t - 2 * h)
        ag_forward(ph, view, h, arrival(i)).wait_recv()
        ag_forward(ph, view, h, arrival(i + 1)).wait_recv()
        return pair_rows(t, arrival)

    def ag_end(ph, view):
        for h in range(2):
            for d in (1, 2, 3):
                ag_direct(ph, view, h, d).wait_send()
            for d in range(4):
                ag_forward(ph, view, h, d).wait_send()
                ra_copy(ph, 4 * h + d).wait_send()
            for d in (1, 2, 3):
                rb_copy(ph, 4 * h + d).wait_send()

    my_half = pl.ds(pl.multiple_of(c * HALF, HALF), HALF)
    other_half = pl.ds(pl.multiple_of((1 - c) * HALF, HALF), HALF)

    def ra_copy(ph, slot):
        return remote(aout.at[slot], ain.at[ph, slot], ra_s.at[ph, slot], ra_r.at[ph, slot], core)

    def rb_copy(ph, slot):
        target = {"x": lax.rem(x + 8 - slot, 4)}
        return remote(bout.at[slot], bin_.at[ph, slot], rb_s.at[ph, slot], rb_r.at[ph, slot], target)

    def rs_begin(ph, slot, value):
        part[slot] = value
        aout[slot] = part[slot, other_half, :].astype(BF)
        ra_copy(ph, slot).start()

    def rs_pass(ph, h, d):
        slot = 4 * h + d
        ra_copy(ph, slot).wait_recv()
        total = part[slot, my_half, :] + ain[ph, slot].astype(F32)

        @pl.when(d == 0)
        def _():
            res[h] = total

        @pl.when(d != 0)
        def _():
            bout[slot] = total.astype(BF)
            rb_copy(ph, slot).start()

    def rs_loop(ph, order, step):
        def pass_pair(t):
            h = t // 2
            for i in range(2):
                rs_pass(ph, h, order(2 * (t - 2 * h) + i))

        def one(t, carry):
            h = t // 2
            value = step(t)
            for i in range(2):
                d = order(2 * (t - 2 * h) + i)
                rs_begin(ph, 4 * h + d, value[i * BLK : (i + 1) * BLK])

            @pl.when(t > 0)
            def _():
                pass_pair(t - 1)

            return carry

        lax.fori_loop(0, 4, one, 0)
        pass_pair(3)

    def rs_end(ph, h):
        total = res[h]
        for d in (1, 3, 2):
            slot = 4 * h + d
            rb_copy(ph, slot).wait_recv()
            total = total + bin_[ph, slot].astype(F32)
        return total

    lanes = lax.broadcasted_iota(jnp.int32, (1, 128), 1) < 64
    head_mask = (
        lanes.astype(F32).astype(BF),
        (1.0 - lanes.astype(F32)).astype(BF),
    )
    first_head = lax.broadcasted_iota(jnp.int32, (128, 128), 1) < 64

    def home_copy(l, src, dst, send, recv):
        return remote(src.at[l], dst.at[s], send.at[l], recv.at[s], {"s": l, "yh": c, "c": yh})

    def home_start(l, src, dst, send, recv):
        @pl.when(mine(l))
        def _():
            dst[s] = src[l]

        @pl.when(jnp.logical_not(mine(l)))
        def _():
            home_copy(l, src, dst, send, recv).start()

    def home_wait(src, dst, send, recv):
        for l in range(2):
            @pl.when(jnp.logical_not(mine(l)))
            def _():
                home_copy(l, src, dst, send, recv).wait_send()
                remote(src.at[l], dst.at[l], send.at[l], recv.at[l], core).wait_recv()

    for h in range(2):
        swap_wait(h)
        ag_start(FA, hbuf.at[0], h)
    relay(0, 4)
    swap_wait(2)
    documents = lax.broadcasted_iota(jnp.int32, (8, SEQ), 0) == segb[...]
    documents = documents.astype(F32).astype(BF)
    put = lax.broadcasted_iota(jnp.int32, (SEQ, SEQ), 1)
    put = put - lax.rem(put, 128) + lax.rem(put, 64) // 32 * 64 + lax.rem(put, 128) // 64 * 32 + lax.rem(put, 32)
    move = lax.broadcasted_iota(jnp.int32, (SEQ, SEQ), 0) == put
    documents = dot_nn(documents, move.astype(F32).astype(BF)).astype(BF)
    bias[...] = jnp.where(dot_tn(documents, documents) > 0.5, 0.0, -1e30)
    relay(0, QKV)
    spread(0, OUT)
    spread(0, UP)
    spread(0, DOWN)
    relay(1, 4)

    @pl.when(diag)
    def _():
        wl_copy(4).wait()

    def forward(l, carry):
        small = sw[l]
        out_b, gain_a, shift_a = small[0:1], small[1:2], small[2:3]
        down_b, gain_b, shift_b = small[3:4], small[4:5], small[5:6]
        view = hbuf.at[l]
        ready(l, QKV)

        def project(t, carry):
            at = ag_pair(FA, view, t)
            rows = load(hbuf, (l,), at)
            q = dot_nn(rows, wq[l, 0]) + sw[l, 6:7, 512:640]
            k = dot_nn(rows, wq[l, 1])
            v = dot_nn(rows, wq[l, 2]) + sw[l, 6:7, 640:768]
            store(qkv, (l, 0), at, q.astype(BF))
            store(qkv, (l, 1), at, k.astype(BF))
            store(qkv, (l, 2), at, v.astype(BF))
            return carry

        lax.fori_loop(0, 4, project, 0)

        @pl.when(l == 1)
        def _():
            relay(1, UP)
            relay(1, DOWN)


        @pl.when(l == 0)
        def _():
            relay(0, OUT)

        ready(l, OUT)

        def attend(t):
            @pl.when(jnp.logical_and(l == 0, t == 1))
            def _():
                for k in (QKV, OUT, UP, DOWN):
                    spread(1, k)

            @pl.when(jnp.logical_and(l == 0, t == 2))
            def _():
                relay(0, UP)

            at = pair_rows(t, reversed_arrival)
            q = load(qkv, (l, 0), at)
            mask = load(bias, (), at)
            keys = qkv[l, 1]
            values = qkv[l, 2]
            heads = []
            for j in range(2):
                scores = dot_nt(q * head_mask[j], keys) * 0.125 + mask
                e = jnp.exp(scores - jnp.max(scores, axis=-1, keepdims=True))
                p = (e * (1.0 / jnp.sum(e, axis=-1, keepdims=True))).astype(BF)
                store(probs, (l, j), at, p)
                heads.append(dot_nn(p, values))
            block = jnp.where(first_head, heads[0], heads[1]).astype(BF)
            store(att, (l,), at, block)
            return dot_nn(block, wo[l])

        rs_loop(FA, reversed_arrival, attend)

        @pl.when(l == 0)
        def _():
            relay(0, DOWN)

        ar_view = arbuf.at[l]
        for h in range(2):
            r1 = hbuf[l, rows_of(x, h, c), :].astype(F32) + rs_end(FA, h) + out_b
            n, scale = normed(r1)
            n1[l, h] = n
            sc1[l, h] = jnp.broadcast_to(scale, (HALF, 128))
            a = n * gain_a + shift_a
            abuf[h] = a
            arbuf[l, rows_of(x, h, c), :] = a.astype(BF)
            ag_start(FM, ar_view, h)
        ag_end(FA, view)
        ready(l, UP)
        ready(l, DOWN)

        def feed(t):
            @pl.when(jnp.logical_and(l == 0, t == 3))
            def _():
                relay(1, QKV)

            at = ag_pair(FM, ar_view, t)
            u = dot_nn(load(arbuf, (l,), at), wu[l]) + sw[l, 6:7, 0:512]
            cdf = 0.5 * (1.0 + lax.erf(u * 0.7071067811865476))
            store(gp, (l,), at, cdf + u * (jnp.exp(-0.5 * u * u) * 0.3989422804014327))
            g = (u * cdf).astype(BF)
            store(gr, (l,), at, g)
            return dot_nn(g, wd[l])

        rs_loop(FM, arrival, feed)
        for h in range(2):
            r2 = abuf[h] + rs_end(FM, h) + down_b
            n, scale = normed(r2)
            n2[l, h] = n
            sc2[l, h] = jnp.broadcast_to(scale, (HALF, 128))
            y = (n * gain_b + shift_b).astype(BF)
            yb[l, h * HALF : (h + 1) * HALF, :] = y

            @pl.when(l == 0)
            def _():
                hbuf[1, rows_of(x, h, c), :] = y
                ag_start(FA, hbuf.at[1], h)

        ag_end(FM, ar_view)

        @pl.when(l == 0)
        def _():
            relay(1, OUT)
            swap_start(3)

        home_start(l, yb, lob, lo_s, lo_r)
        return carry

    lax.fori_loop(0, 2, forward, 0)

    def gz_copy(l, k, d):
        src = at_piece(grads[k], k, lax.rem(z + d, 4), (l,))
        return remote(src, zrecv[k].at[l, d - 1], gz_s.at[l, k, d], gz_r.at[l, k, d], z_dev(d))

    def gz_start(l, k):
        for d in (1, 3, 2):
            gz_copy(l, k, d).start()

    def gy_copy(l, k):
        slot = 2 * lax.rem(yh + 2 - c, 2) + lax.rem(s + 2 - l, 2)
        return remote(
            yout[k].at[l], yrecv[k].at[slot - 1], gy_s.at[l, k], gy_r.at[k, slot], {"s": l, "yh": c}
        )

    def gy_start(l, k):
        total = at_piece(grads[k], k, z, (l,))[...].astype(F32)
        for d in (1, 3, 2):
            gz_copy(l, k, d).wait_recv()
            total = total + zrecv[k][l, d - 1].astype(F32)
        yout[k][l] = total.astype(BF)

        @pl.when(jnp.logical_not(mine(l)))
        def _():
            gy_copy(l, k).start()

    def fz_copy(k, d):
        piece = at_piece(final[k], k, z)
        return remote(piece, piece, fz_s.at[k, d], fz_r.at[k, d], z_dev(d))

    def fc_copy(k, d):
        piece = at_piece(final[k], k, lax.rem(z + 4 - d, 4))
        return remote(piece, piece, fc_s.at[k, d], fc_r.at[k, d], core)

    def fz_start(k):
        @pl.when(diag)
        def _():
            total = yout[k][s].astype(F32)
            for i in (1, 2, 3):
                remote(
                    yrecv[k].at[i - 1], yrecv[k].at[i - 1], gy_s.at[0, k], gy_r.at[k, i], core
                ).wait_recv()
                total = total + yrecv[k][i - 1].astype(F32)
            at_piece(final[k], k, z)[...] = total.astype(BF)
            for d in (1, 3, 2):
                fz_copy(k, d).start()
            fc_copy(k, 0).start()

    def fc_start(k):
        @pl.when(diag)
        def _():
            for d in (1, 3, 2):
                piece = at_piece(final[k], k, lax.rem(z + 4 - d, 4))
                remote(piece, piece, fz_s.at[k, d], fz_r.at[k, d], z_dev(d)).wait_recv()
                fc_copy(k, d).start()

    def out_start(k):
        @pl.when(jnp.logical_not(diag))
        def _():
            for d in range(4):
                fc_copy(k, d).wait_recv()

        pltpu.make_async_copy(final[k], outs[k], st.at[k]).start()

    def sx_copy(l, d):
        return remote(gsb.at[l], sx.at[l, x], sx_s.at[l, d], sx_r.at[l, d], {"x": lax.rem(x + d, 4)})

    def sc_copy(l):
        return remote(sc.at[l, c], sc.at[l, c], sc_s.at[l], sc_r.at[l], core)

    def sz_copy(l, d):
        return remote(sz.at[l, z], sz.at[l, z], sz_s.at[l, d], sz_r.at[l, d], z_dev(d))

    def sy_copy(l, i):
        block = sy.at[l, 2 * yh + s]
        return remote(block, block, sy_s.at[l, i], sy_r.at[l, i], y_dev(i))

    def small_x(l):
        sx[l, x] = gsb[l]
        for d in (1, 3, 2):
            sx_copy(l, d).start()

    def small_core(l):
        for d in (1, 3, 2):
            sx_copy(l, d).wait_recv()
        sc[l, c] = ((sx[l, 0] + sx[l, 1]) + sx[l, 2]) + sx[l, 3]
        sc[l, c, 6:7, :] = gsb[l, 6:7, :]
        sc_copy(l).start()

    def small_z(l):
        sc_copy(l).wait_recv()
        sz[l, z] = sc[l, 0] + sc[l, 1]
        sz[l, z, 6:7, :] = sc[l, 0, 6:7, :]
        sz[l, z, 7:8, :] = sc[l, 1, 6:7, :]
        for d in (1, 3, 2):
            sz_copy(l, d).start()

    def small_y(l):
        for d in (1, 3, 2):
            sz_copy(l, d).wait_recv()
        sy[l, 2 * yh + s] = ((sz[l, 0] + sz[l, 1]) + sz[l, 2]) + sz[l, 3]
        for i in (1, 3, 2):
            sy_copy(l, i).start()

    def small_end():
        for l in range(2):
            for i in (1, 3, 2):
                sy_copy(l, i).wait_recv()
        gsout[...] = ((sy[s, 0] + sy[s, 1]) + sy[s, 2]) + sy[s, 3]

        @pl.when(yh == 1)
        def _():
            gsout[6:7, :] = gsout[7:8, :]

    swap_wait(3)

    def input_grad(l, h):
        low = (abuf[h] + rs_end(BA, h)).astype(BF)
        dhb[l, h * HALF : (h + 1) * HALF, :] = low
        return low.astype(F32)

    def grads_qkv(l):
        def some(i, carry):
            cols = pl.ds(pl.multiple_of(i * 128, 128), 128)
            rows = hbuf[l, :, cols]
            for j in range(3):
                g0[l, j, cols, :] = dot_tn(rows, dx[j]).astype(BF)
            return carry

        lax.fori_loop(0, 8, some, 0)
        gz_start(l, QKV)

    def grads_out(l):
        g1[l] = dot_tn(att[l], dprbuf[...]).astype(BF)
        gz_start(l, OUT)

    def grads_down(l):
        def some(i, carry):
            cols = pl.ds(pl.multiple_of(i * 128, 128), 128)
            g3[l, cols, :] = dot_tn(gr[l, :, cols], dmbuf[...]).astype(BF)
            return carry

        lax.fori_loop(0, 4, some, 0)
        gz_start(l, DOWN)

    def grads_up(l):
        def some(i, carry):
            cols = pl.ds(pl.multiple_of(i * 128, 128), 128)
            g2[l, cols, :] = dot_tn(arbuf[l, :, cols], dur[...]).astype(BF)
            return carry

        lax.fori_loop(0, 8, some, 0)
        gz_start(l, UP)

    def backward(step_index, carry):
        l = 1 - step_index
        small = sw[l]
        gain_a, gain_b = small[1:2], small[4:5]
        gsb[l] = jnp.zeros((8, D), F32)
        for h in range(2):
            @pl.when(l == 1)
            def _():
                dyb[...] = cotb[h * HALF : (h + 1) * HALF, :].astype(F32)

            @pl.when(l == 0)
            def _():
                dyb[...] = input_grad(1, h)

            dy = dyb[...]
            n = n2[l, h]
            dr2 = norm_back(dy, gain_b, n, sc2[l, h, :, 0:1])
            dmbuf[rows_of(x, h, c), :] = dr2.astype(BF)
            ag_start(BM, dmbuf, h)
            abuf[h] = dr2
            gsb[l, 4:5, :] += col_sum(dy * n)
            gsb[l, 5:6, :] += col_sum(dy)
            gsb[l, 3:4, :] += col_sum(dr2)

            @pl.when(l == 0)
            def _():
                if h == 0:
                    grads_qkv(1)
                else:
                    grads_out(1)
                    small_z(1)
                    ag_end(BA, dprbuf)
                    home_start(1, dhb, igb, ig_s, ig_r)

        def feed_back(t):
            at = ag_pair(BM, dmbuf, t)
            dg = dot_nt(load(dmbuf, (), at), wd[l])
            du = dg * load(gp, (l,), at)
            gsb[l, 6:7, 0:512] += col_sum(du)
            low = du.astype(BF)
            store(dur, (), at, low)
            return dot_nt(low, wu[l])

        rs_loop(BM, arrival, feed_back)
        for h in range(2):
            da = abuf[h] + rs_end(BM, h)
            n = n1[l, h]
            dr1 = norm_back(da, gain_a, n, sc1[l, h, :, 0:1])
            dprbuf[rows_of(x, h, c), :] = dr1.astype(BF)
            ag_start(BA, dprbuf, h)
            abuf[h] = dr1
            gsb[l, 1:2, :] += col_sum(da * n)
            gsb[l, 2:3, :] += col_sum(da)
            gsb[l, 0:1, :] += col_sum(dr1)
            if h == 0:
                grads_down(l)
            else:
                grads_up(l)
        ag_end(BM, dmbuf)
        dacc[...] = jnp.zeros_like(dacc)

        @pl.when(l == 0)
        def _():
            small_y(1)
            for k in (DOWN, UP):
                gy_start(1, k)

        def attend_back(t, carry):
            at = ag_pair(BA, dprbuf, t)
            grad = dot_nt(load(dprbuf, (), at), wo[l]).astype(BF)
            q = load(qkv, (l, 0), at)
            keys = qkv[l, 1]
            values = qkv[l, 2]
            heads = []
            dk = dacc[0]
            dv = dacc[1]
            for j in range(2):
                own = grad * head_mask[j]
                low_p = load(probs, (l, j), at)
                p = low_p.astype(F32)
                dp = dot_nt(own, values)
                ds = (p * (dp - jnp.sum(p * dp, axis=-1, keepdims=True))).astype(BF)
                heads.append(dot_nn(ds, keys))
                dk = dk + dot_tn(ds, q * head_mask[j])
                dv = dv + dot_tn(low_p, own)
            dacc[0] = dk
            dacc[1] = dv
            dq = (jnp.where(first_head, heads[0], heads[1]) * 0.125).astype(BF)
            store(dx, (0,), at, dq)
            gsb[l, 6:7, 512:640] += col_sum(dq.astype(F32))
            return carry

        lax.fori_loop(0, 4, attend_back, 0)
        dx[1] = (dacc[0] * 0.125).astype(BF)
        dv = dacc[1].astype(BF)
        dx[2] = dv
        gsb[l, 6:7, 640:768] = col_sum(dv.astype(F32))
        small_x(l)

        @pl.when(l == 0)
        def _():
            grads_qkv(0)
            grads_out(0)
            for k in (QKV, OUT):
                gy_start(1, k)

        def input_back(t):
            at = pair_rows(t, reversed_arrival)
            return (
                dot_nt(load(dx, (0,), at), wq[l, 0])
                + dot_nt(load(dx, (1,), at), wq[l, 1])
                + dot_nt(load(dx, (2,), at), wq[l, 2])
            )

        rs_loop(BA, reversed_arrival, input_back)
        small_core(l)
        return carry

    lax.fori_loop(0, 2, backward, 0)
    for k in (DOWN, UP):
        gy_start(0, k)
    small_z(0)
    for h in range(2):
        input_grad(0, h)
    ag_end(BA, dprbuf)
    home_start(0, dhb, igb, ig_s, ig_r)
    small_y(0)

    for k in (DOWN, UP):
        fz_start(k)
    for k in (QKV, OUT):
        gy_start(0, k)
    for k in (DOWN, UP):
        fc_start(k)
    for k in (QKV, OUT):
        fz_start(k)
    home_wait(yb, lob, lo_s, lo_r)
    lo_out = pltpu.make_async_copy(lob, lo, st.at[5])
    lo_out.start()
    home_wait(dhb, igb, ig_s, ig_r)
    ig_out = pltpu.make_async_copy(igb, ig, st.at[6])
    ig_out.start()
    small_end()
    small_out = pltpu.make_async_copy(gsout, gs, st.at[4])
    small_out.start()
    for k in (DOWN, UP):
        out_start(k)
    for k in (QKV, OUT):
        fc_start(k)
    for k in (QKV, OUT):
        out_start(k)

    @pl.when(diag)
    def _():
        for k in range(5):
            for i in (1, 2, 3):
                for j in range(1 if k == 4 else 2):
                    wy_copy(k, i, j).wait_send()

    for l in range(2):
        for k in range(4):
            @pl.when(jnp.logical_not(mine(l)))
            def _():
                for d in (1, 3):
                    wz_copy(l, k, d).wait_send()
                gy_copy(l, k).wait_send()

            for d in (1, 2, 3):
                gz_copy(l, k, d).wait_send()

        for d in (1, 2, 3):
            sx_copy(l, d).wait_send()
            sz_copy(l, d).wait_send()
            sy_copy(l, d).wait_send()
        sc_copy(l).wait_send()

    @pl.when(diag)
    def _():
        for k in range(4):
            for d in (1, 2, 3):
                fz_copy(k, d).wait_send()
            for d in range(4):
                fc_copy(k, d).wait_send()

    small_out.wait()
    lo_out.wait()
    ig_out.wait()
    for k in range(4):
        pltpu.make_async_copy(final[k], outs[k], st.at[k]).wait()


WSHAPES = ((3, D, 128), (128, D), (D, FFS), (FFS, D))
PSHAPES = ((3, 256, 128), (32, D), (256, FFS), (128, D))


def run(*operands):
    vm = pltpu.VMEM
    scratch = [vm((8, D), F32), vm((2, 8, SEQ), jnp.int32)]
    scratch += [vm((2, *shape), BF) for shape in WSHAPES]
    scratch += [vm((2, 8, D), F32)]
    scratch += [vm((2, SEQ, D), BF)] * 2 + [vm((SEQ, D), BF)] * 2
    scratch += [vm((4, 8, HALF, D), BF)] * 2 + [vm((8, HALF, D), BF)] * 2 + [vm((8, BLK, D), F32)]
    scratch += [
        vm((2, 3, SEQ, 128), BF),
        vm((2, SEQ, 128), BF),
        vm((2, 2, SEQ, SEQ), BF),
        vm((2, SEQ, FFS), F32),
        vm((2, SEQ, FFS), BF),
        vm((2, 2, HALF, D), F32),
        vm((2, 2, HALF, D), F32),
        vm((2, 2, HALF, 128), F32),
        vm((2, 2, HALF, 128), F32),
        vm((2, HALF, D), F32),
        vm((2, HALF, D), F32),
        vm((HALF, D), F32),
    ]
    scratch += [
        vm((8, SEQ), jnp.int32),
        vm((SEQ, SEQ), F32),
        vm((BLK, D), BF),
        vm((SEQ, FFS), BF),
        vm((2, SEQ, 128), F32),
        vm((3, SEQ, 128), BF),
    ]
    scratch += [vm((2, BLK, D), BF)] * 4 + [vm((2, 8, D), F32)]
    scratch += [vm((2, n, 8, D), F32) for n in (4, 2, 4, 4)] + [vm((8, D), F32)]
    scratch += [vm((2, *shape), BF) for shape in WSHAPES]
    scratch += [vm((2, 3, *shape), BF) for shape in PSHAPES]
    scratch += [vm((2, *shape), BF) for shape in PSHAPES]
    scratch += [vm((3, *shape), BF) for shape in PSHAPES]
    scratch += [vm(shape, BF) for shape in WSHAPES]
    dma = pltpu.SemaphoreType.DMA
    scratch += [dma((4,)), dma((4,)), dma((5, 4, 2)), dma((2, 5, 2)), dma((2, 4, 4)), dma((2, 4, 4)), dma((5,))]
    scratch += [dma((4, 8))] * 8
    scratch += [dma((2,))] * 4
    scratch += [dma((2, 4, 4)), dma((2, 4, 4)), dma((2, 4)), dma((4, 4))]
    scratch += [dma((4, 4))] * 4 + [dma((7,))]
    scratch += [dma((2, 4))] * 2 + [dma((2,))] * 2 + [dma((2, 4))] * 4
    any_space = pl.BlockSpec(memory_space=pl.ANY)
    in_vmem = pl.BlockSpec(memory_space=pltpu.VMEM)
    return pl.pallas_call(
        kernel,
        out_shape=[
            jax.ShapeDtypeStruct((2, BLK, D), BF),
            jax.ShapeDtypeStruct((2, BLK, D), BF),
            *(jax.ShapeDtypeStruct(shape, BF) for shape in WSHAPES),
            jax.ShapeDtypeStruct((8, D), F32),
        ],
        in_specs=[any_space] * 2 + [in_vmem] + [any_space] * 4 + [in_vmem] * 8,
        out_specs=[any_space] * 7,
        scratch_shapes=scratch,
        compiler_params=pltpu.CompilerParams(
            collective_id=0, has_side_effects=True, vmem_limit_bytes=60 * 1024 * 1024
        ),
    )(*operands)


def finish_kernel(lo, ig, gq, go, gu, gd, gs, lo_o, ig_o, gq_o, qv_o, go_o, ob_o, ga_o, sa_o, gu_o, ub_o, gd_o, db_o, gb_o, sb_o):
    lo_o[0, :, 0] = lo[...]
    ig_o[0, :, 0] = ig[...]
    gq_o[0] = gq[...].astype(F32)
    go_o[0] = go[...].astype(F32)
    gu_o[0] = gu[...].astype(F32)
    gd_o[0] = gd[...].astype(F32)
    for row, ref in enumerate((ob_o, ga_o, sa_o, db_o, gb_o, sb_o)):
        ref[...] = gs[row : row + 1, :]
    ub_o[...] = gs[6:7, 0:512]
    qv_o[0, 0:1, :] = gs[6:7, 512:640]
    qv_o[0, 1:2, :] = gs[6:7, 640:768]


FSHAPES = ((3, 512, 128), (64, D), (512, FFS), (256, D))


def finish(lo, ig, *rest):
    steps = 2
    row = ((1, D), lambda i: (0, 0))
    wide = ((2, BLK // steps, D), lambda i: (0, i, 0))
    wide_out = ((1, 2, 1, BLK // steps, D), lambda i: (0, 0, 0, i, 0))
    wmaps = ((lambda i: (0, i, 0)), (lambda i: (i, 0)), (lambda i: (i, 0)), (lambda i: (i, 0)))
    omaps = ((lambda i: (0, 0, i, 0)),) + ((lambda i: (0, i, 0)),) * 3
    gq_o, go_o, gu_o, gd_o = (((1, *shape), m) for shape, m in zip(FSHAPES, omaps))
    specs_in = [wide, wide, *zip(FSHAPES, wmaps), ((8, D), lambda i: (0, 0))]
    specs_out = [
        wide_out, wide_out, gq_o, ((1, 2, 128), lambda i: (0, 0, 0)), go_o, row, row, row,
        gu_o, ((1, FFS), lambda i: (0, 0)), gd_o, row, row, row,
    ]
    full = [
        ((1, 2, 1, BLK, D), BF), ((1, 2, 1, BLK, D), BF), ((1, 3, D, 128), F32), ((1, 2, 128), F32),
        ((1, 128, D), F32), ((1, D), F32), ((1, D), F32), ((1, D), F32), ((1, D, FFS), F32),
        ((1, FFS), F32), ((1, FFS, D), F32), ((1, D), F32), ((1, D), F32), ((1, D), F32),
    ]
    return pl.pallas_call(
        finish_kernel,
        grid=(steps,),
        out_shape=[jax.ShapeDtypeStruct(*leaf) for leaf in full],
        in_specs=[pl.BlockSpec(*spec) for spec in specs_in],
        out_specs=[pl.BlockSpec(*spec) for spec in specs_out],
        compiler_params=pltpu.CompilerParams(vmem_limit_bytes=60 * 1024 * 1024),
    )(lo, ig, *rest)


def local(
    inputs, segments, qkv_weight, qv_bias, out_weight, out_bias, gain_one, shift_one,
    up_weight, up_bias, down_weight, down_bias, gain_two, shift_two, cotangent,
):
    results = run(
        inputs[:, 0], cotangent[:, 0], segments,
        qkv_weight[0], out_weight[0], up_weight[0], down_weight[0],
        out_bias, gain_one, shift_one, down_bias, gain_two, shift_two, up_bias, qv_bias,
    )
    return tuple(finish(*results))


def solution(mesh):
    fine = Mesh(mesh.devices.reshape(2, 4, 2, 4, 2), ("s", "x", "yh", "z", "c"))
    t = ("x", "yh")
    dp = ("z", "c")
    return jax.shard_map(
        local,
        mesh=fine,
        in_specs=(
            P(None, dp, t, None),
            P(None, dp, None),
            P("s", None, None, t),
            P("s", None, t),
            P("s", t, None),
            P("s", None),
            P("s", None),
            P("s", None),
            P("s", None, t),
            P("s", t),
            P("s", t, None),
            P("s", None),
            P("s", None),
            P("s", None),
            P(None, dp, t, None),
        ),
        out_specs=(
            P("s", None, dp, t, None),
            P("s", None, dp, t, None),
            P("s", None, None, t),
            P("s", None, t),
            P("s", t, None),
            P("s", None),
            P("s", None),
            P("s", None),
            P("s", None, t),
            P("s", t),
            P("s", t, None),
            P("s", None),
            P("s", None),
            P("s", None),
        ),
        check_vma=False,
    )
```
